768 devices in a mesh: fn: 24 (over z, core), blk: 32 (over y, x).
Axes of the slice: x: 4, y: 8, z: 12, core: 2. Of those that a mesh axis runs over, the one named last changes fastest.
Arguments:
- orbitals: bfloat16 [6144, 32768], P('fn', 'blk'), may hold values from -1 to 1
- potential: float32 [24, 32768], P('fn', 'blk'), may hold values from 0.5 to 2
- zone_of: int32 [6144, 1], P('fn'), may hold values from 0 to 23; in each aligned block of 256 rows (0 to 255, 256 to 511, ...) at most 24 rows name the same one
- chem_shift: float32 [1], replicated, may hold values from 0.9 to 1.6
Outputs:
- intersection: float32 [24, 576, 576], P('fn', 'blk')
- hamiltonian: float32 [24, 576, 576], P('fn', 'blk')
- kernel: float32 [24, 576, 576], P('fn', 'blk')
The draws below stay inside these ranges and needn't reach their ends.
Inputs may be any that keep to these rules, and one draw needn't show every extreme that they name: `zone_of`: among the 256 functions of one index of fn (aligned blocks of rows) no zone is named more than 24 times, and in some block one zone is named exactly 24 times; every zone is named somewhere.
All inputs are finite; a program needn't handle non-finite values.
Results may differ from the reference program's by a relative error of at most 0.00074.
Values may be sent and summed in bfloat16 or wider, within the bound.
A program may use at most 32 MiB of HBM per device.

```python
import math
import jax
import jax.numpy as jnp
import numpy as np
from jax import lax

FUNC_DEV = 256
SLOTS = 576
CAP = 24
NFUNC = 6144
ZPTS = 32768
N_FN = 24


def draw_orbitals(key, part):
    key = jax.random.fold_in(key, 11)
    keys = jax.random.split(key, 4)
    spread = float(ZPTS) / float(FUNC_DEV)
    centers = jax.random.uniform(keys[0], (NFUNC, 1), jnp.float32, 0.0, float(ZPTS))
    points = jnp.arange(ZPTS, dtype=jnp.float32)[None, :]
    offset = jnp.abs(points - centers)
    offset = jnp.minimum(offset, float(ZPTS) - offset)
    envelope = jnp.exp(-0.5 * (offset / spread) ** 2)
    noise = jnp.clip(jax.random.normal(keys[1], (NFUNC, ZPTS), jnp.float32), -5.0, 5.0)
    amplitude = jnp.clip(jax.random.normal(keys[2], (NFUNC, 1), jnp.float32), -2.5, 2.5)
    common = jnp.clip(jax.random.normal(keys[3], (1, ZPTS), jnp.float32), -3.5, 3.5)
    row_scale = jnp.ones((NFUNC, 1), jnp.float32)
    noise_scale = math.sqrt(0.85 / float(ZPTS))
    bump_scale = math.sqrt(0.15 / (spread * math.sqrt(math.pi)))
    values = row_scale * noise_scale * noise + bump_scale * amplitude * envelope * common
    values = jnp.clip(values, -1.0, 1.0)
    return values.astype(jnp.bfloat16)


def draw_potential(key, part):
    key = jax.random.fold_in(key, 23)
    keys = jax.random.split(key, 2)
    width = max(1, ZPTS // FUNC_DEV)
    count = (ZPTS + width - 1) // width
    high_share = 0.5
    jitter_top = 0.25
    high_blocks = jax.random.uniform(keys[0], (N_FN, count), jnp.float32) < high_share
    high_points = jnp.repeat(high_blocks, width, axis=1)[:, :ZPTS]
    jitter = jax.random.uniform(keys[1], (N_FN, ZPTS), jnp.float32, 0.0, jitter_top)
    values = jnp.where(high_points, 2.0 * jnp.exp(-jitter), 0.5 * jnp.exp(jitter))
    return values.astype(jnp.float32)


def deal_out(key, own, number, rows, amount, top, limit, slope):
    order = jax.random.permutation(key, amount)
    packed, ordinary = load_shares(amount, rows * top, limit, slope, True), load_shares(amount, rows * top, limit, slope, False)
    places = jnp.arange(amount)

    def named(sizes, rotation):
        used = int((sizes > 0).sum())
        fixed = max(1, used // 4)
        passed = fixed + (places - fixed + rotation * (used - fixed)) % max(1, amount - fixed)
        return jnp.zeros((amount,), jnp.int32).at[order[jnp.where(places < fixed, places, passed)]].set(jnp.asarray(sizes, jnp.int32))

    sizes = jnp.where(number % 4 == 0, named(packed, number // 4), named(ordinary, number - number // 4 - 1))
    mixed = jax.random.permutation(jax.random.fold_in(own, 3), amount)
    source_of, sink = mixed[0:amount // 2 * 2:2], mixed[1:amount // 2 * 2:2]
    slack = jnp.minimum(sizes[source_of] - 1, limit - sizes[sink]) // 2
    slack = jnp.where((source_of == order[0]) | (sink == order[0]) | (sizes[sink] == 0), 0, jnp.maximum(slack, 0))
    passed = jax.random.randint(jax.random.fold_in(own, 4), (amount // 2,), 0, 1 << 20) % (slack + 1)
    sizes = sizes.at[source_of].add(-passed).at[sink].add(passed)
    members = jnp.searchsorted(jnp.cumsum(sizes), jnp.arange(rows * top), side="right").astype(jnp.int32)
    table = members.reshape(top, rows).T
    table = table[jax.random.permutation(jax.random.fold_in(own, 1), rows)]
    rotation = jax.random.randint(jax.random.fold_in(own, 2), (rows, 1), 0, top)
    return jnp.take_along_axis(table, (jnp.arange(top)[None, :] + rotation) % top, axis=1)


def load_shares(count, total, reach, skew, full):
    weights = [(1 << 20) // math.isqrt(standing ** skew) + 1 for standing in range(1, count + 1)]
    largest = reach if full else min(reach, max(-(-total // count), total * weights[0] // sum(weights)))
    least = 1 if total - largest >= count - 1 else 0
    given, spare = [largest] + [least] * (count - 1), total - largest - least * (count - 1)
    while spare > 0:
        free = [i for i in range(1, count) if given[i] < largest] or [i for i in range(1, count) if given[i] < reach]
        pool, budget = sum([weights[i] for i in free]), spare
        for i in free:
            addition = min(reach - given[i], max(1, budget * weights[i] // pool), spare)
            given[i] = given[i] + addition
            spare = spare - addition
    return np.array(given)


def setup_inputs(seed: int = 0) -> dict:
    key_list = jax.random.split(jax.random.key(seed), 5)
    orbitals = draw_orbitals(jax.random.fold_in(key_list[4], 71), 0)
    potential = draw_potential(jax.random.fold_in(key_list[4], 71), 0)
    zone_of_keys = jax.random.split(jax.random.fold_in(key_list[2], 1), NFUNC // FUNC_DEV)
    zone_of_turns = jax.random.permutation(jax.random.fold_in(key_list[2], 3), NFUNC // FUNC_DEV)
    zone_of = jax.vmap(lambda own, number: deal_out(jax.random.fold_in(key_list[2], 2), own, number, FUNC_DEV, N_FN, 1, CAP, 2))(zone_of_keys, zone_of_turns).reshape((NFUNC, 1))
    chem_shift = jnp.clip(jax.random.uniform(key_list[3], (1,), jnp.float32, 0.9, 1.6), 0.9, 1.6)
    return {"orbitals": orbitals, "potential": potential, "zone_of": zone_of, "chem_shift": chem_shift}


def reference(orbitals, potential, zone_of, chem_shift):
    zone_ids = zone_of[:, 0].astype(jnp.int32)
    onehot = (zone_ids[:, None] == jnp.arange(N_FN, dtype=jnp.int32)[None, :]).astype(jnp.int32)
    grouped = onehot.reshape(N_FN, FUNC_DEV, N_FN)
    rank_in = jnp.sum((jnp.cumsum(grouped, axis=1).astype(jnp.int32) - grouped) * grouped, axis=2).reshape(-1).astype(jnp.int32)
    owners = (jnp.arange(N_FN * FUNC_DEV, dtype=jnp.int32) // FUNC_DEV).astype(jnp.int32)
    slot_ids = (owners * CAP + rank_in).astype(jnp.int32)
    slot_table = jnp.zeros((N_FN, SLOTS), jnp.int32).at[zone_ids, slot_ids].set(jnp.arange(N_FN * FUNC_DEV, dtype=jnp.int32))
    present = jnp.zeros((N_FN, SLOTS), jnp.float32).at[zone_ids, slot_ids].set(1.0)
    mu_value = chem_shift[0]
    highest = lax.Precision.HIGHEST

    def zone_block(zone_item):
        fn_rows, marks, zone_pot = zone_item
        coeffs = jnp.where(marks[:, None] > 0, orbitals[fn_rows], jnp.zeros((), orbitals.dtype))
        weighted = (zone_pot[None, :] * coeffs.astype(jnp.float32)).astype(jnp.bfloat16)
        intersection = jnp.dot(coeffs, coeffs.T, preferred_element_type=jnp.float32)
        hamiltonian = jnp.dot(coeffs, weighted.T, preferred_element_type=jnp.float32)
        diagonal = jnp.eye(SLOTS, dtype=jnp.float32) * marks[None, :]
        start = 0.5 * diagonal - 0.5 * (hamiltonian - mu_value * intersection)
        product = jnp.dot(start, intersection, precision=highest, preferred_element_type=jnp.float32)
        square = jnp.dot(product, start, precision=highest, preferred_element_type=jnp.float32)
        cubed = jnp.dot(product, square, precision=highest, preferred_element_type=jnp.float32)
        return intersection, hamiltonian, 3.0 * square - 2.0 * cubed

    intersection, hamiltonian, kernel = lax.map(zone_block, (slot_table, present, potential))
    return (intersection, hamiltonian, kernel)
```

```python
import jax
import jax.numpy as jnp
from jax import lax
from jax.experimental import pallas as pl
from jax.experimental.pallas import tpu as pltpu
from jax.sharding import PartitionSpec as P

SLOTS = 576
WIDE = 640
LANES = 128
NX = 4
CORES = 2
BIG = 2.0**100
BF16 = jnp.bfloat16
F32 = jnp.float32

STRIP_ROWS = [SLOTS - LANES * j for j in range(5)]
STRIP_AT = [sum(STRIP_ROWS[:j]) for j in range(5)]
TRIANGLE = sum(STRIP_ROWS)


def wrap(value, n):
    return lax.rem(value + n, n)


def rows(start, count):
    return pl.ds(pl.multiple_of(start, 8), count)


def near_first(k):
    return ((k + 1) // 2) * (2 * lax.rem(k, 2) - 1)


def first_part(count):
    return (count // 2 + 7) // 8 * 8


def split(value):
    high = value.astype(BF16)
    return high, (value - high.astype(F32)).astype(BF16)


def times(left, right_high, right_low):
    high, low = split(left)
    count = left.shape[0]
    both = jnp.dot(
        jnp.concatenate([high, low], axis=0), right_high[...], preferred_element_type=F32
    )
    return both[:count] + both[count:] + jnp.dot(high, right_low[...], preferred_element_type=F32)


class Ring:
    def __init__(self, n, me, device, base, size):
        self.n, self.me, self.device, self.base, self.size = n, me, device, base, size
        self.hops = n // 2
        self.part = first_part(size)

    def at(self, offset):
        return self.base + wrap(self.me + offset, self.n) * self.size


def cut(ring, way, whole):
    if whole:
        return 0, ring.size
    return (0, ring.part) if way > 0 else (ring.part, ring.size - ring.part)


def ring_sum(ring, data, landing, send_sem, recv_sem):
    copies = {}

    def send(t, way):
        skip, count = cut(ring, way, t > 0)
        d = 0 if way > 0 else 1
        copies[t, way] = pltpu.make_async_remote_copy(
            src_ref=data.at[rows(ring.at(way * (ring.hops - t)) + skip, count)],
            dst_ref=landing.at[d, t, pl.ds(skip, count)],
            send_sem=send_sem.at[d, t],
            recv_sem=recv_sem.at[d, t],
            device_id=ring.device(wrap(ring.me + way, ring.n)),
        )
        copies[t, way].start()

    def add(t, way):
        copies[t, way].wait_recv()
        skip, count = cut(ring, way, t > 0)
        here = rows(ring.at(way * (ring.hops - t - 1)) + skip, count)
        data[here, :] += landing[0 if way > 0 else 1, t, pl.ds(skip, count), :]

    def step(t):
        def run():
            for way in (1, -1):
                if t > 0:
                    add(t - 1, way)
                if t < ring.hops:
                    send(t, way)

        return run

    return [step(t) for t in range(ring.hops + 1)], copies


def ring_gather(ring, data, send_sem, recv_sem):
    sent = []

    def copy(t, way, offset):
        skip, count = cut(ring, way, t < ring.hops - 1)
        d = 0 if way > 0 else 1
        here = data.at[rows(ring.at(offset) + skip, count)]
        return pltpu.make_async_remote_copy(
            src_ref=here,
            dst_ref=here,
            send_sem=send_sem.at[d, t],
            recv_sem=recv_sem.at[d, t],
            device_id=ring.device(wrap(ring.me + way, ring.n)),
        )

    def step(t):
        def run():
            for way in (1, -1):
                if t > 0:
                    copy(t - 1, way, -way * t).wait_recv()
                if t < ring.hops:
                    out = copy(t, way, -way * t)
                    out.start()
                    sent.append(out)

        return run

    return [step(t) for t in range(ring.hops + 1)], sent


def direct_sum(ring, data, total, landing, send_sem, recv_sem):
    copies = []

    def start():
        for k in range(1, ring.n):
            copies.append(
                pltpu.make_async_remote_copy(
                    src_ref=data.at[rows(ring.at(k), ring.size)],
                    dst_ref=landing.at[k - 1],
                    send_sem=send_sem.at[k - 1],
                    recv_sem=recv_sem.at[k - 1],
                    device_id=ring.device(wrap(ring.me + k, ring.n)),
                )
            )
            copies[-1].start()

    def finish():
        here = rows(ring.at(0), ring.size)
        value = data[here, :]
        for k in range(1, ring.n):
            copies[k - 1].wait_recv()
            value = value + landing[k - 1]
        total[here, :] = value

    return start, finish, copies


def direct_gather(ring, data, send_sem, recv_sem):
    sent = []

    def copy(k, offset):
        here = data.at[rows(ring.at(offset), ring.size)]
        return pltpu.make_async_remote_copy(
            src_ref=here,
            dst_ref=here,
            send_sem=send_sem.at[k - 1],
            recv_sem=recv_sem.at[k - 1],
            device_id=ring.device(wrap(ring.me + k, ring.n)),
        )

    def start():
        for k in range(1, ring.n):
            sent.append(copy(k, 0))
            sent[-1].start()

    def finish():
        for k in range(1, ring.n):
            copy(k, -k).wait_recv()

    return start, finish, sent


def kernel(
    n_fn, ny, size_a, size_b,
    zone_ref, orb_ref, pot_ref, mu_ref, s_out, h_out, k_out,
    send, recv, coeffs, weighted, present, part, gath,
    land_ya, land_xa, land_xb, land_yb,
    s_full, h_full, l_full, s_high, s_low, l_high, l_low, l_rows,
    z_send, z_recv, sum_ya, sum_xa, sum_xb, sum_yb, get_ya, get_xa, get_xb, get_yb,
):
    cap = SLOTS // n_fn
    nz = n_fn // CORES
    me = lax.axis_index("fn")
    blk = lax.axis_index("blk")
    my_z, core = me // CORES, lax.rem(me, CORES)
    y, x = blk // NX, lax.rem(blk, NX)

    def along_y(pos):
        return {"blk": pos * NX + x}

    def along_x(pos):
        return {"blk": y * NX + pos}

    def fn_index(dz, dc):
        return wrap(my_z + dz, nz) * CORES + lax.rem(core + dc, CORES)

    barrier = pltpu.get_barrier_semaphore()

    @pl.loop(1, n_fn)
    def _(k):
        pl.semaphore_signal(barrier, inc=1, device_id={"fn": wrap(me + k - n_fn, n_fn)})

    for k in range(1, ny):
        pl.semaphore_signal(barrier, inc=1, device_id=along_y(wrap(y + k, ny)))
    for k in range(1, NX):
        pl.semaphore_signal(barrier, inc=1, device_id=along_x(wrap(x + k, NX)))

    funcs = orb_ref.shape[0]
    zones = zone_ref[...]
    onehot = (zones == lax.broadcasted_iota(jnp.int32, (n_fn, funcs), 0)).astype(F32)
    earlier = (
        lax.broadcasted_iota(jnp.int32, (funcs, funcs), 0)
        < lax.broadcasted_iota(jnp.int32, (funcs, funcs), 1)
    ).astype(F32)
    before = jnp.dot(onehot.astype(BF16), earlier.astype(BF16), preferred_element_type=F32)
    rank = jnp.sum(before * onehot, axis=0, keepdims=True).astype(jnp.int32)
    target = zones * cap + rank
    selector = (target == lax.broadcasted_iota(jnp.int32, (SLOTS, funcs), 0)).astype(F32)
    filled = jnp.sum(selector, axis=1, keepdims=True) > 0.5
    selector = selector.astype(BF16)
    slab = orb_ref.shape[1]
    for c0 in range(0, slab, 256):
        slotted = jnp.dot(selector, orb_ref[:, c0 : c0 + 256], preferred_element_type=F32)
        if c0 == 0:
            slotted = jnp.where(filled, slotted, BIG)
        for zone in range(n_fn):
            send[zone, :, c0 : c0 + 256] = slotted[zone * cap : (zone + 1) * cap].astype(BF16)

    pl.semaphore_wait(barrier, n_fn - 1 + ny - 1 + NX - 1)

    def z_copy(k, dc, dz_from):
        dz = near_first(k)
        q = CORES * k + dc - 1
        to = fn_index(dz, dc)
        return pltpu.make_async_remote_copy(
            src_ref=send.at[to],
            dst_ref=recv.at[fn_index(dz_from * dz, dc) if dz_from else me],
            send_sem=z_send.at[q],
            recv_sem=z_recv.at[q],
            device_id={"fn": to},
        )

    z_copy(0, 1, 0).start()

    @pl.loop(1, nz)
    def _(k):
        for dc in range(CORES):
            z_copy(k, dc, 0).start()

    recv[me] = send[me]
    coeffs[SLOTS:, :] = jnp.zeros((WIDE - SLOTS, slab), BF16)
    weighted[SLOTS:, :] = jnp.zeros((WIDE - SLOTS, slab), BF16)
    if part.shape[0] > 2 * TRIANGLE:
        part[2 * TRIANGLE :, :] = jnp.zeros((part.shape[0] - 2 * TRIANGLE, LANES), F32)
    potential = pot_ref[...]

    def unpack(dz):
        chip = wrap(my_z - dz, nz)
        value = jnp.concatenate(
            [recv[chip * CORES + c].astype(F32) for c in range(CORES)], axis=0
        )
        marks = value[:, :1] < 0.5 * BIG
        value = jnp.where(marks, value, 0.0)
        here = pl.ds(pl.multiple_of(chip * (CORES * cap), 16), CORES * cap)
        coeffs[here, :] = value.astype(BF16)
        weighted[here, :] = (potential * value).astype(BF16)
        present[here, :] = jnp.broadcast_to(marks.astype(F32), (CORES * cap, LANES))

    z_copy(0, 1, -1).wait_recv()
    unpack(0)

    @pl.loop(1, nz)
    def _(k):
        for dc in range(CORES):
            z_copy(k, dc, -1).wait_recv()
        unpack(near_first(k))

    def outer(left, right, j, width):
        return lax.dot_general(
            left[LANES * j : SLOTS, :],
            right[LANES * j : LANES * j + width, :],
            (((1,), (1,)), ((), ())),
            preferred_element_type=F32,
        )

    def store(value, at, j):
        part[at + STRIP_AT[j] : at + STRIP_AT[j] + STRIP_ROWS[j], :] = value

    for j, width in ((0, 256), (2, 256), (4, 128)):
        gram = outer(coeffs, coeffs, j, width)
        ham = 0.5 * (outer(coeffs, weighted, j, width) + outer(weighted, coeffs, j, width))
        for at, value in ((0, gram), (TRIANGLE, ham)):
            store(value[:, :LANES], at, j)
            if width > LANES:
                store(value[LANES:, LANES:], at, j + 1)

    base_b = ny * NX * size_a
    ring_ya = Ring(ny, y, along_y, 0, NX * size_a)
    ring_xa = Ring(NX, x, along_x, y * (NX * size_a), size_a)
    ring_xb = Ring(NX, x, along_x, base_b, ny * size_b)
    ring_yb = Ring(ny, y, along_y, base_b + x * (ny * size_b), size_b)
    ya, sent_ya = ring_sum(ring_ya, part, land_ya, sum_ya.at[0], sum_ya.at[1])
    xb, sent_xb = ring_sum(ring_xb, part, land_xb, sum_xb.at[0], sum_xb.at[1])
    xa_start, xa_finish, sent_xa = direct_sum(
        ring_xa, part, gath, land_xa, sum_xa.at[0], sum_xa.at[1]
    )
    yb_start, yb_finish, sent_yb = direct_sum(
        ring_yb, part, gath, land_yb, sum_yb.at[0], sum_yb.at[1]
    )
    ga_start, ga_finish, sent_ga = direct_gather(ring_xa, gath, get_xa.at[0], get_xa.at[1])
    gb_start, gb_finish, sent_gb = direct_gather(ring_yb, gath, get_yb.at[0], get_yb.at[1])
    gya, sent_gya = ring_gather(ring_ya, gath, get_ya.at[0], get_ya.at[1])
    gxb, sent_gxb = ring_gather(ring_xb, gath, get_xb.at[0], get_xb.at[1])

    def merged(a, b):
        keyed = [((i + 0.5) / len(a), 0, s) for i, s in enumerate(a)]
        keyed += [((i + 0.5) / len(b), 1, s) for i, s in enumerate(b)]
        for _, _, s in sorted(keyed, key=lambda item: item[:2]):
            s()

    merged(ya[:-1], xb[:-1])
    xb[-1]()
    yb_start()
    ya[-1]()
    xa_start()
    xa_finish()
    ga_start()
    yb_finish()
    gb_start()
    ga_finish()
    gya[0]()
    gb_finish()
    gxb[0]()
    merged(gya[1:], gxb[1:])

    mu = mu_ref[0]
    eye = (
        lax.broadcasted_iota(jnp.int32, (LANES, LANES), 0)
        == lax.broadcasted_iota(jnp.int32, (LANES, LANES), 1)
    ).astype(F32)
    for i in range(5):
        high = min(LANES, SLOTS - LANES * i)
        for j in range(i + 1):
            at = STRIP_AT[j] + LANES * (i - j)
            s_block = gath[at : at + high, :]
            h_block = gath[TRIANGLE + at : TRIANGLE + at + high, :]
            l_block = -0.5 * (h_block - mu * s_block)
            if i == j:
                l_block = l_block + 0.5 * eye[:high] * present[LANES * i : LANES * i + high, :]
            for block, full in ((s_block, s_full), (h_block, h_full), (l_block, l_full)):
                if high < LANES:
                    block = jnp.concatenate([block, jnp.zeros((LANES - high, LANES), F32)], axis=0)
                full[LANES * i : LANES * (i + 1), LANES * j : LANES * (j + 1)] = block
                if i > j:
                    full[LANES * j : LANES * (j + 1), LANES * i : LANES * (i + 1)] = block.T

    first = blk * s_out.shape[1]
    l_rows[...] = jnp.zeros(l_rows.shape, F32)
    for i in range(s_out.shape[1]):
        s_out[0, i : i + 1, :] = s_full[pl.ds(first + i, 1), :][:, :SLOTS]
        h_out[0, i : i + 1, :] = h_full[pl.ds(first + i, 1), :][:, :SLOTS]
        l_rows[i : i + 1, :] = l_full[pl.ds(first + i, 1), :]
    for i in range(5):
        here = slice(LANES * i, LANES * (i + 1))
        s_high[here, :], s_low[here, :] = split(s_full[here, :])
        l_high[here, :], l_low[here, :] = split(l_full[here, :])

    product = times(l_rows[...], s_high, s_low)
    square = times(product, l_high, l_low)
    cubed = times(times(square, s_high, s_low), l_high, l_low)
    k_out[0] = (3.0 * square - 2.0 * cubed)[: k_out.shape[1], :SLOTS]

    z_copy(0, 1, 0).wait_send()

    @pl.loop(1, nz)
    def _(k):
        for dc in range(CORES):
            z_copy(k, dc, 0).wait_send()

    sent = list(sent_ya.values()) + list(sent_xb.values())
    for copy in sent + sent_xa + sent_yb + sent_ga + sent_gb + sent_gya + sent_gxb:
        copy.wait_send()


def on_device(orbitals, potential, zone_of, chem_shift):
    n_fn = lax.axis_size("fn")
    n_blk = lax.axis_size("blk")
    ny = n_blk // NX
    cap = SLOTS // n_fn
    funcs, slab = orbitals.shape
    count = SLOTS // n_blk
    each = -(-2 * TRIANGLE // (n_blk * 8)) * 8
    size_a = each * 6 // 13 // 8 * 8
    size_b = each - size_a

    def sems(*shape):
        return pltpu.SemaphoreType.DMA((2,) + shape)

    hy, hx = ny // 2, NX // 2
    out = jax.ShapeDtypeStruct((1, count, SLOTS), F32)
    vmem = pl.BlockSpec(memory_space=pltpu.VMEM)

    def body(*refs):
        kernel(n_fn, ny, size_a, size_b, *refs)

    return pl.pallas_call(
        body,
        out_shape=(out, out, out),
        in_specs=[vmem, vmem, vmem, pl.BlockSpec(memory_space=pltpu.SMEM)],
        out_specs=(vmem, vmem, vmem),
        scratch_shapes=[
            pltpu.VMEM((n_fn, cap, slab), BF16),
            pltpu.VMEM((n_fn, cap, slab), BF16),
            pltpu.VMEM((WIDE, slab), BF16),
            pltpu.VMEM((WIDE, slab), BF16),
            pltpu.VMEM((SLOTS, LANES), F32),
            pltpu.VMEM((n_blk * each, LANES), F32),
            pltpu.VMEM((n_blk * each, LANES), F32),
            pltpu.VMEM((2, hy, NX * size_a, LANES), F32),
            pltpu.VMEM((NX - 1, size_a, LANES), F32),
            pltpu.VMEM((2, hx, ny * size_b, LANES), F32),
            pltpu.VMEM((ny - 1, size_b, LANES), F32),
            pltpu.VMEM((WIDE, WIDE), F32),
            pltpu.VMEM((WIDE, WIDE), F32),
            pltpu.VMEM((WIDE, WIDE), F32),
            pltpu.VMEM((WIDE, WIDE), BF16),
            pltpu.VMEM((WIDE, WIDE), BF16),
            pltpu.VMEM((WIDE, WIDE), BF16),
            pltpu.VMEM((WIDE, WIDE), BF16),
            pltpu.VMEM((-(-count // 16) * 16, WIDE), F32),
            pltpu.SemaphoreType.DMA((n_fn - 1,)),
            pltpu.SemaphoreType.DMA((n_fn - 1,)),
            sems(2, hy),
            sems(NX - 1),
            sems(2, hx),
            sems(ny - 1),
            sems(2, hy),
            sems(NX - 1),
            sems(2, hx),
            sems(ny - 1),
        ],
        compiler_params=pltpu.CompilerParams(
            collective_id=0, has_side_effects=True, vmem_limit_bytes=48 * 1024 * 1024
        ),
    )(zone_of.reshape(1, funcs), orbitals, potential, chem_shift)


def solution(mesh):
    placed = (P("fn", "blk"), P("fn", "blk"), P("fn", None), P())
    return jax.shard_map(
        on_device,
        mesh=mesh,
        in_specs=placed,
        out_specs=(P("fn", "blk", None), P("fn", "blk", None), P("fn", "blk", None)),
        check_vma=False,
    )
```

```python
import jax
import jax.numpy as jnp
from jax import lax
from jax.experimental import pallas as pl
from jax.experimental.pallas import tpu as pltpu
from jax.sharding import PartitionSpec as P

SLOTS = 576
WIDE = 640
LANES = 128
NX = 4
CORES = 2
BIG = 2.0**100
BF16 = jnp.bfloat16
F32 = jnp.float32

TILES = [
    [(0, 0, 336), (1, 128, 336), (2, 256, 336)],
    [(0, 336, 432), (1, 336, 432), (2, 336, 432), (3, 384, 432)],
    [(0, 432, 528), (1, 432, 528), (2, 432, 528), (3, 432, 528)],
    [(0, 528, 576), (1, 528, 576), (2, 528, 576), (3, 528, 576), (4, 512, 576)],
]


def wrap(value, n):
    return lax.rem(value + n, n)


def rows(start, count):
    return pl.ds(pl.multiple_of(start, 8), count)


def split(value):
    high = value.astype(BF16)
    return high, (value - high.astype(F32)).astype(BF16)


def times(left, right_high, right_low):
    high, low = split(left)
    count = left.shape[0]
    both = jnp.dot(
        jnp.concatenate([high, low], axis=0), right_high[...], preferred_element_type=F32
    )
    return both[:count] + both[count:] + jnp.dot(high, right_low[...], preferred_element_type=F32)


class Ring:
    def __init__(self, n, me, device, base, size):
        self.n, self.me, self.device, self.base, self.size = n, me, device, base, size

    def at(self, offset):
        return self.base + wrap(self.me + offset, self.n) * self.size


def far_first(n):
    return sorted(range(1, n), key=lambda k: -min(k, n - k))


def direct_sum(ring, data, total, landing, send_sem, recv_sem):
    copies = []

    def start():
        for k in far_first(ring.n):
            copies.append(
                pltpu.make_async_remote_copy(
                    src_ref=data.at[rows(ring.at(k), ring.size)],
                    dst_ref=landing.at[k - 1],
                    send_sem=send_sem.at[k - 1],
                    recv_sem=recv_sem.at[k - 1],
                    device_id=ring.device(wrap(ring.me + k, ring.n)),
                )
            )
            copies[-1].start()

    def finish():
        here = rows(ring.at(0), ring.size)
        value = data[here, :]
        for copy, k in zip(copies, far_first(ring.n)):
            copy.wait_recv()
            value = value + landing[k - 1]
        total[here, :] = value

    return start, finish, copies


def direct_gather(ring, data, send_sem, recv_sem):
    sent = []

    def copy(k, offset):
        here = data.at[rows(ring.at(offset), ring.size)]
        return pltpu.make_async_remote_copy(
            src_ref=here,
            dst_ref=here,
            send_sem=send_sem.at[k - 1],
            recv_sem=recv_sem.at[k - 1],
            device_id=ring.device(wrap(ring.me + k, ring.n)),
        )

    def start():
        for k in far_first(ring.n):
            sent.append(copy(k, 0))
            sent[-1].start()

    def finish():
        for k in far_first(ring.n):
            copy(k, -k).wait_recv()

    return start, finish, sent


class Batch:
    def __init__(self, n_x, n_y, x, y, along_x, along_y, size, refs):
        part, gath, land_x, land_y, sum_x, sum_y, get_y, get_x = refs
        self.part, self.gath = part, gath
        ring_x = Ring(n_x, x, along_x, 0, n_y * size)
        ring_y = Ring(n_y, y, along_y, x * (n_y * size), size)
        stages = [
            direct_sum(ring_x, part, part, land_x, sum_x.at[0], sum_x.at[1]),
            direct_sum(ring_y, part, gath, land_y, sum_y.at[0], sum_y.at[1]),
            direct_gather(ring_y, gath, get_y.at[0], get_y.at[1]),
            direct_gather(ring_x, gath, get_x.at[0], get_x.at[1]),
        ]
        self.starts = [s[0] for s in stages]
        self.finishes = [s[1] for s in stages]
        self.sent = [s[2] for s in stages]
        self.stage = 0

    def begin(self):
        self.starts[0]()

    def advance(self):
        self.finishes[self.stage]()
        self.stage += 1
        if self.stage < len(self.starts):
            self.starts[self.stage]()

    def drain(self):
        for copies in self.sent:
            for copy in copies:
                copy.wait_send()


def kernel(
    n_fn, ny, sizes,
    zone_hbm, orb_hbm, pot_hbm, mu_ref, packed,
    zone_ref, orb_ref, pot_ref, in_sem, send, recv, coeffs, weighted, present, place,
    s_full, h_full, l_full, s_high, s_low, l_high, l_low, l_rows,
    z_send, z_recv, *batch_refs,
):
    cap = SLOTS // n_fn
    nz = n_fn // CORES
    deep = CORES * cap
    me = lax.axis_index("fn")
    blk = lax.axis_index("blk")
    my_z, core = me // CORES, lax.rem(me, CORES)
    y, x = blk // NX, lax.rem(blk, NX)

    def along_y(pos):
        return {"blk": pos * NX + x}

    def along_x(pos):
        return {"blk": y * NX + pos}

    def fn_index(dz, dc):
        return wrap(my_z + dz, nz) * CORES + lax.rem(core + dc, CORES)

    barrier = pltpu.get_barrier_semaphore()

    @pl.loop(1, n_fn)
    def _(k):
        pl.semaphore_signal(barrier, inc=1, device_id={"fn": wrap(me + k - n_fn, n_fn)})

    for k in range(1, ny):
        pl.semaphore_signal(barrier, inc=1, device_id=along_y(wrap(y + k, ny)))
    for k in range(1, NX):
        pl.semaphore_signal(barrier, inc=1, device_id=along_x(wrap(x + k, NX)))

    loads = [
        pltpu.make_async_copy(src, dst, in_sem.at[i])
        for i, (src, dst) in enumerate(
            ((zone_hbm, zone_ref), (orb_hbm, orb_ref), (pot_hbm, pot_ref))
        )
    ]
    for load in loads:
        load.start()
    coeffs[...] = jnp.zeros(coeffs.shape, BF16)
    weighted[...] = jnp.zeros(weighted.shape, BF16)

    loads[0].wait()
    funcs = orb_ref.shape[0]
    slab = orb_ref.shape[1]
    zones = zone_ref[...]
    onehot = (zones == lax.broadcasted_iota(jnp.int32, (n_fn, funcs), 0)).astype(F32)
    earlier = (
        lax.broadcasted_iota(jnp.int32, (funcs, funcs), 0)
        < lax.broadcasted_iota(jnp.int32, (funcs, funcs), 1)
    ).astype(F32)
    before = jnp.dot(onehot.astype(BF16), earlier.astype(BF16), preferred_element_type=F32)
    rank = jnp.sum(before * onehot, axis=0, keepdims=True).astype(jnp.int32)
    target = zones * cap + rank
    selector = (target == lax.broadcasted_iota(jnp.int32, (SLOTS, funcs), 0)).astype(F32)
    filled = jnp.sum(selector, axis=1, keepdims=True) > 0.5
    selector = selector.astype(BF16)
    wide = min(256, slab)
    loads[1].wait()
    for c0 in range(0, slab, wide):
        slotted = jnp.dot(selector, orb_ref[:, c0 : c0 + wide], preferred_element_type=F32)
        if c0 == 0:
            slotted = jnp.where(filled, slotted, BIG)
        for zone in range(n_fn):
            send[zone, :, c0 : c0 + wide] = slotted[zone * cap : (zone + 1) * cap].astype(BF16)
    loads[2].wait()

    pl.semaphore_wait(barrier, n_fn - 1 + ny - 1 + NX - 1)

    def near(k):
        return (k + 1) // 2 * (1 if k % 2 else -1)

    z_waiting = []

    def z_copy(k, dc, arriving):
        q = CORES * k + dc - 1
        to = fn_index(near(k), dc)
        return pltpu.make_async_remote_copy(
            src_ref=send.at[to],
            dst_ref=recv.at[fn_index(-near(k), dc) if arriving else me],
            send_sem=z_send.at[q],
            recv_sem=z_recv.at[q],
            device_id={"fn": to},
        )

    def z_start(*chips):
        for k in chips:
            for dc in range(0 if k else 1, CORES):
                z_copy(k, dc, False).start()
                z_waiting.append((k, dc))

    def z_left(*chips):
        for k, dc in [item for item in z_waiting if item[0] in chips]:
            z_copy(k, dc, False).wait_send()
            z_waiting.remove((k, dc))

    def unpack(*chips):
        for k in chips:
            for dc in range(0 if k else 1, CORES):
                z_copy(k, dc, True).wait_recv()
            chip = wrap(my_z - near(k), nz)
            value = jnp.concatenate(
                [recv[chip * CORES + c].astype(F32) for c in range(CORES)], axis=0
            )
            marks = value[:, :1] < 0.5 * BIG
            value = jnp.where(marks, value, 0.0)
            here = slice(k * deep, (k + 1) * deep)
            coeffs[here, :] = value.astype(BF16)
            weighted[here, :] = (pot_ref[...] * value).astype(BF16)
            present[here, :] = jnp.broadcast_to(marks.astype(F32), (deep, LANES))

    batches = [
        Batch(NX, ny, x, y, along_x, along_y, size, batch_refs[8 * i : 8 * i + 8])
        for i, size in enumerate(sizes)
    ]

    def share(i):
        part = batches[i].part
        tiles = TILES[i]
        low = min(r0 for _, r0, _ in tiles)
        high = max(r1 for _, _, r1 in tiles)
        span = LANES * (tiles[-1][0] + 1)
        mine, mine_w = coeffs[low:high, :], weighted[low:high, :]
        count = high - low
        over = (((1,), (1,)), ((), ()))
        at = 0
        for c0 in range(0, span, 256):
            c1 = min(c0 + 256, span)
            both = lax.dot_general(
                jnp.concatenate([mine, mine_w], axis=0), coeffs[c0:c1, :], over,
                preferred_element_type=F32,
            )
            other = lax.dot_general(mine, weighted[c0:c1, :], over, preferred_element_type=F32)
            gram, ham = both[:count], 0.5 * (both[count:] + other)
            for j, r0, r1 in tiles:
                if c0 <= LANES * j < c1:
                    cols = slice(LANES * j - c0, LANES * (j + 1) - c0)
                    part[at : at + r1 - r0, :] = gram[r0 - low : r1 - low, cols]
                    at += r1 - r0
                    part[at : at + r1 - r0, :] = ham[r0 - low : r1 - low, cols]
                    at += r1 - r0
        if at < part.shape[0]:
            part[at:, :] = jnp.zeros((part.shape[0] - at, LANES), F32)
        batches[i].begin()

    def collect(i):
        at = 0
        for j, r0, r1 in TILES[i]:
            cols = slice(LANES * j, LANES * (j + 1))
            s_full[r0:r1, cols] = batches[i].gath[at : at + r1 - r0, :]
            at += r1 - r0
            h_full[r0:r1, cols] = batches[i].gath[at : at + r1 - r0, :]
            at += r1 - r0

    def advance(*order):
        for i in order:
            batches[i].advance()
            if batches[i].stage == 4:
                collect(i)

    def place_columns():
        p = lax.broadcasted_iota(jnp.int32, (WIDE, 1), 0)
        k = p // deep
        dz = (k + 1) // 2 * (2 * lax.rem(k, 2) - 1)
        slot = lax.rem(my_z - dz + nz, nz) * deep + p - k * deep
        slot = jnp.where(p < SLOTS, slot, p)
        place[...] = (slot == lax.broadcasted_iota(jnp.int32, (WIDE, WIDE), 1)).astype(F32).astype(BF16)

    z_start(0, 1, 2, 3, 4)
    recv[me] = send[me]
    place_columns()
    present[SLOTS:, :] = jnp.zeros((WIDE - SLOTS, LANES), F32)
    s_full[SLOTS:, :] = jnp.zeros((WIDE - SLOTS, WIDE), F32)
    h_full[SLOTS:, :] = jnp.zeros((WIDE - SLOTS, WIDE), F32)
    l_rows[...] = jnp.zeros(l_rows.shape, F32)
    unpack(0)
    z_left(1, 2)
    z_start(5, 6)
    unpack(1, 2)
    z_left(3, 4)
    z_start(7, 8)
    unpack(3, 4)
    z_left(5, 6)
    z_start(9, 10)
    unpack(5, 6)
    share(0)
    z_left(7, 8)
    z_start(11)
    advance(0)
    unpack(7, 8)
    share(1)
    advance(0, 1)
    unpack(9, 10)
    share(2)
    advance(0, 1, 2, 1)
    unpack(11)
    share(3)
    advance(0, 2, 3, 1, 2, 3, 2, 3, 3)

    mu = mu_ref[0]
    down = lax.broadcasted_iota(jnp.int32, (LANES, LANES), 0)
    across = lax.broadcasted_iota(jnp.int32, (LANES, LANES), 1)
    for i in range(5):
        here = slice(LANES * i, LANES * (i + 1))
        for j in range(i + 1):
            there = slice(LANES * j, LANES * (j + 1))
            s_block, h_block = s_full[here, there], h_full[here, there]
            if i == j:
                s_block = jnp.where(down >= across, s_block, s_block.T)
                h_block = jnp.where(down >= across, h_block, h_block.T)
            l_block = -0.5 * (h_block - mu * s_block)
            if i == j:
                l_block = l_block + jnp.where(down == across, 0.5 * present[here, :], 0.0)
                s_full[here, there] = s_block
                h_full[here, there] = h_block
            l_full[here, there] = l_block
            if i > j:
                s_full[there, here] = s_block.T
                h_full[there, here] = h_block.T
                l_full[there, here] = l_block.T

    count = packed.shape[1]
    room = l_rows.shape[1]
    for i in range(count):
        slot = blk * count + i
        chip = slot // deep
        dz = wrap(my_z - chip, nz)
        far = (dz + nz // 2 - 1) // nz
        k = (1 - far) * (2 * dz - (dz + nz - 1) // nz) + far * (2 * nz - 2 * dz)
        row = pl.ds(k * deep + slot - chip * deep, 1)
        l_rows[0, i : i + 1, :] = l_full[row, :]
        l_rows[1, i : i + 1, :] = s_full[row, :]
        l_rows[2, i : i + 1, :] = h_full[row, :]
    for i in range(5):
        here = slice(LANES * i, LANES * (i + 1))
        s_high[here, :], s_low[here, :] = split(s_full[here, :])
        l_high[here, :], l_low[here, :] = split(l_full[here, :])

    product = times(l_rows[0], s_high, s_low)
    square = times(product, l_high, l_low)
    cubed = times(times(square, s_high, s_low), l_high, l_low)

    result = jnp.concatenate([l_rows[1], l_rows[2], 3.0 * square - 2.0 * cubed], axis=0)
    high, rest = result.astype(BF16), result - result.astype(BF16).astype(F32)
    middle, low = split(rest)
    placed = jnp.dot(
        jnp.concatenate([high, middle, low], axis=0), place[...], preferred_element_type=F32
    )
    placed = placed[: 3 * room] + placed[3 * room : 6 * room] + placed[6 * room :]
    for i in range(3):
        packed[i] = placed[i * room : i * room + count, :SLOTS].reshape(count, 1, SLOTS)

    z_left(*range(nz))
    for batch in batches:
        batch.drain()


def hand_out(packed, *outs):
    for i, out in enumerate(outs):
        out[...] = packed[i]


def on_device(orbitals, potential, zone_of, chem_shift):
    n_fn = lax.axis_size("fn")
    n_blk = lax.axis_size("blk")
    ny = n_blk // NX
    cap = SLOTS // n_fn
    funcs, slab = orbitals.shape
    count = SLOTS // n_blk
    sizes = [
        -(-2 * sum(r1 - r0 for _, r0, r1 in tiles) // (n_blk * 8)) * 8 for tiles in TILES
    ]
    batch_scratch = []
    for size in sizes:
        batch_scratch += [
            pltpu.VMEM((n_blk * size, LANES), F32),
            pltpu.VMEM((n_blk * size, LANES), F32),
            pltpu.VMEM((max(1, NX - 1), ny * size, LANES), F32),
            pltpu.VMEM((ny - 1, size, LANES), F32),
        ] + [pltpu.SemaphoreType.DMA((2, max(1, n - 1))) for n in (NX, ny, ny, NX)]

    out = jax.ShapeDtypeStruct((count, 1, SLOTS), F32)
    vmem = pl.BlockSpec(memory_space=pltpu.VMEM)
    hbm = pl.BlockSpec(memory_space=pltpu.HBM)

    def body(*refs):
        kernel(n_fn, ny, sizes, *refs)

    packed = pl.pallas_call(
        body,
        out_shape=jax.ShapeDtypeStruct((3, count, 1, SLOTS), F32),
        in_specs=[hbm, hbm, hbm, pl.BlockSpec(memory_space=pltpu.SMEM)],
        out_specs=vmem,
        scratch_shapes=[
            pltpu.VMEM((1, funcs), jnp.int32),
            pltpu.VMEM((funcs, slab), BF16),
            pltpu.VMEM((1, slab), F32),
            pltpu.SemaphoreType.DMA((3,)),
            pltpu.VMEM((n_fn, cap, slab), BF16),
            pltpu.VMEM((n_fn, cap, slab), BF16),
            pltpu.VMEM((WIDE, slab), BF16),
            pltpu.VMEM((WIDE, slab), BF16),
            pltpu.VMEM((WIDE, LANES), F32),
            pltpu.VMEM((WIDE, WIDE), BF16),
            pltpu.VMEM((WIDE, WIDE), F32),
            pltpu.VMEM((WIDE, WIDE), F32),
            pltpu.VMEM((WIDE, WIDE), F32),
            pltpu.VMEM((WIDE, WIDE), BF16),
            pltpu.VMEM((WIDE, WIDE), BF16),
            pltpu.VMEM((WIDE, WIDE), BF16),
            pltpu.VMEM((WIDE, WIDE), BF16),
            pltpu.VMEM((3, -(-count // 16) * 16, WIDE), F32),
            pltpu.SemaphoreType.DMA((n_fn - 1,)),
            pltpu.SemaphoreType.DMA((n_fn - 1,)),
            *batch_scratch,
        ],
        compiler_params=pltpu.CompilerParams(
            collective_id=0, has_side_effects=True, vmem_limit_bytes=60 * 1024 * 1024
        ),
    )(zone_of.reshape(1, funcs), orbitals, potential, chem_shift)
    results = pl.pallas_call(
        hand_out,
        out_shape=(out, out, out),
        in_specs=[vmem],
        out_specs=(vmem, vmem, vmem),
    )(packed)
    return tuple(jnp.transpose(result, (1, 0, 2)) for result in results)


def solution(mesh):
    placed = (P("fn", "blk"), P("fn", "blk"), P("fn", None), P())
    return jax.shard_map(
        on_device,
        mesh=mesh,
        in_specs=placed,
        out_specs=(P("fn", "blk", None), P("fn", "blk", None), P("fn", "blk", None)),
        check_vma=False,
    )
```

```python
import jax
import jax.numpy as jnp
from jax import lax
from jax.experimental import pallas as pl
from jax.experimental.pallas import tpu as pltpu
from jax.sharding import PartitionSpec as P

SLOTS = 576
WIDE = 640
LANES = 128
NX = 4
CORES = 2
BIG = 2.0**100
BF16 = jnp.bfloat16
F32 = jnp.float32

TILES = [
    [(0, 0, 240), (1, 128, 240)],
    [(0, 240, 336), (1, 240, 336), (2, 272, 336)],
    [(0, 336, 432), (1, 336, 432), (2, 256, 272), (2, 336, 432), (3, 384, 432)],
    [(0, 432, 528), (1, 432, 528), (2, 432, 528), (3, 432, 528)],
    [(0, 528, 576), (1, 528, 576), (2, 528, 576), (3, 528, 576), (4, 512, 576)],
]


def wrap(value, n):
    return lax.rem(value + n, n)


def rows(start, count):
    return pl.ds(pl.multiple_of(start, 8), count)


def split(value):
    high = value.astype(BF16)
    return high, (value - high.astype(F32)).astype(BF16)


def times(left, right_high, right_low):
    high, low = split(left)
    count = left.shape[0]
    both = jnp.dot(
        jnp.concatenate([high, low], axis=0), right_high[...], preferred_element_type=F32
    )
    return both[:count] + both[count:] + jnp.dot(high, right_low[...], preferred_element_type=F32)


class Ring:
    def __init__(self, n, me, device, base, size):
        self.n, self.me, self.device, self.base, self.size = n, me, device, base, size

    def at(self, offset):
        return self.base + wrap(self.me + offset, self.n) * self.size


def far_first(n):
    return sorted(range(1, n), key=lambda k: -min(k, n - k))


def direct_sum(ring, data, total, landing, send_sem, recv_sem):
    copies = []

    def start():
        for k in far_first(ring.n):
            copies.append(
                pltpu.make_async_remote_copy(
                    src_ref=data.at[rows(ring.at(k), ring.size)],
                    dst_ref=landing.at[k - 1],
                    send_sem=send_sem.at[k - 1],
                    recv_sem=recv_sem.at[k - 1],
                    device_id=ring.device(wrap(ring.me + k, ring.n)),
                )
            )
            copies[-1].start()

    def finish():
        here = rows(ring.at(0), ring.size)
        value = data[here, :]
        for copy, k in zip(copies, far_first(ring.n)):
            copy.wait_recv()
            value = value + landing[k - 1]
        total[here, :] = value

    return start, finish, copies


def direct_gather(ring, data, send_sem, recv_sem):
    sent = []

    def copy(k, offset):
        here = data.at[rows(ring.at(offset), ring.size)]
        return pltpu.make_async_remote_copy(
            src_ref=here,
            dst_ref=here,
            send_sem=send_sem.at[k - 1],
            recv_sem=recv_sem.at[k - 1],
            device_id=ring.device(wrap(ring.me + k, ring.n)),
        )

    def start():
        for k in far_first(ring.n):
            sent.append(copy(k, 0))
            sent[-1].start()

    def finish():
        for k in far_first(ring.n):
            copy(k, -k).wait_recv()

    return start, finish, sent


class Batch:
    def __init__(self, n_x, n_y, x, y, along_x, along_y, size, refs):
        part, gath, land_x, land_y, sum_x, sum_y, get_y, get_x = refs
        self.part, self.gath = part, gath
        ring_x = Ring(n_x, x, along_x, 0, n_y * size)
        ring_y = Ring(n_y, y, along_y, x * (n_y * size), size)
        stages = [
            direct_sum(ring_x, part, part, land_x, sum_x.at[0], sum_x.at[1]),
            direct_sum(ring_y, part, gath, land_y, sum_y.at[0], sum_y.at[1]),
            direct_gather(ring_y, gath, get_y.at[0], get_y.at[1]),
            direct_gather(ring_x, gath, get_x.at[0], get_x.at[1]),
        ]
        self.starts = [s[0] for s in stages]
        self.finishes = [s[1] for s in stages]
        self.sent = [s[2] for s in stages]
        self.stage = 0

    def begin(self):
        self.starts[0]()

    def advance(self):
        self.finishes[self.stage]()
        self.stage += 1
        if self.stage < len(self.starts):
            self.starts[self.stage]()

    def drain(self):
        for copies in self.sent:
            for copy in copies:
                copy.wait_send()


def kernel(
    n_fn, ny, sizes,
    zone_hbm, orb_hbm, pot_hbm, mu_ref, packed,
    zone_ref, orb_ref, pot_ref, in_sem, send, recv, coeffs, weighted, present, place,
    s_full, h_full, l_full, s_high, s_low, l_high, l_low, l_rows,
    z_send, z_recv, *batch_refs,
):
    cap = SLOTS // n_fn
    nz = n_fn // CORES
    deep = CORES * cap
    me = lax.axis_index("fn")
    blk = lax.axis_index("blk")
    my_z, core = me // CORES, lax.rem(me, CORES)
    y, x = blk // NX, lax.rem(blk, NX)

    def along_y(pos):
        return {"blk": pos * NX + x}

    def along_x(pos):
        return {"blk": y * NX + pos}

    def fn_index(dz, dc):
        return wrap(my_z + dz, nz) * CORES + lax.rem(core + dc, CORES)

    barrier = pltpu.get_barrier_semaphore()

    @pl.loop(1, n_fn)
    def _(k):
        pl.semaphore_signal(barrier, inc=1, device_id={"fn": wrap(me + k - n_fn, n_fn)})

    for k in range(1, ny):
        pl.semaphore_signal(barrier, inc=1, device_id=along_y(wrap(y + k, ny)))
    for k in range(1, NX):
        pl.semaphore_signal(barrier, inc=1, device_id=along_x(wrap(x + k, NX)))

    loads = [
        pltpu.make_async_copy(src, dst, in_sem.at[i])
        for i, (src, dst) in enumerate(
            ((zone_hbm, zone_ref), (orb_hbm, orb_ref), (pot_hbm, pot_ref))
        )
    ]
    for load in loads:
        load.start()
    loads[0].wait()
    funcs = orb_ref.shape[0]
    slab = orb_ref.shape[1]
    zones = zone_ref[...]
    onehot = (zones == lax.broadcasted_iota(jnp.int32, (n_fn, funcs), 0)).astype(F32)
    earlier = (
        lax.broadcasted_iota(jnp.int32, (funcs, funcs), 0)
        < lax.broadcasted_iota(jnp.int32, (funcs, funcs), 1)
    ).astype(F32)
    before = jnp.dot(onehot.astype(BF16), earlier.astype(BF16), preferred_element_type=F32)
    rank = jnp.sum(before * onehot, axis=0, keepdims=True).astype(jnp.int32)
    target = zones * cap + rank
    loads[1].wait()
    loads[2].wait()

    def near(k):
        return (k + 1) // 2 * (1 if k % 2 else -1)

    z_waiting = []

    def z_copy(k, dc, arriving):
        q = CORES * k + dc - 1
        to = fn_index(near(k), dc)
        return pltpu.make_async_remote_copy(
            src_ref=send.at[to],
            dst_ref=recv.at[fn_index(-near(k), dc) if arriving else me],
            send_sem=z_send.at[q],
            recv_sem=z_recv.at[q],
            device_id={"fn": to},
        )

    def z_start(chips, cores):
        for k in chips:
            for dc in cores:
                z_copy(k, dc, False).start()
                z_waiting.append((k, dc))

    def z_left(chips, cores):
        for k in chips:
            for dc in cores:
                z_copy(k, dc, False).wait_send()
                z_waiting.remove((k, dc))

    def fill(*chips):
        for k in chips:
            chip = wrap(my_z + near(k), nz)
            slot = lax.broadcasted_iota(jnp.int32, (deep, funcs), 0) + chip * deep
            selector = (target == slot).astype(F32)
            filled = jnp.sum(selector, axis=1, keepdims=True) > 0.5
            block = jnp.dot(selector.astype(BF16), orb_ref[...], preferred_element_type=F32)
            block = jnp.where(filled, block, BIG)
            for c in range(CORES):
                send[chip * CORES + c] = block[c * cap : (c + 1) * cap].astype(BF16)

    def unpack(*chips):
        for k in chips:
            for dc in range(0 if k else 1, CORES):
                z_copy(k, dc, True).wait_recv()
            chip = wrap(my_z - near(k), nz)
            value = jnp.concatenate(
                [recv[chip * CORES + c].astype(F32) for c in range(CORES)], axis=0
            )
            marks = value[:, :1] < 0.5 * BIG
            value = jnp.where(marks, value, 0.0)
            here = slice(k * deep, (k + 1) * deep)
            coeffs[here, :] = value.astype(BF16)
            weighted[here, :] = (pot_ref[...] * value).astype(BF16)
            present[here, :] = jnp.broadcast_to(marks.astype(F32), (deep, LANES))

    batches = [
        Batch(NX, ny, x, y, along_x, along_y, size, batch_refs[8 * i : 8 * i + 8])
        for i, size in enumerate(sizes)
    ]

    def share(i):
        part = batches[i].part
        tiles = TILES[i]
        low = min(r0 for _, r0, _ in tiles)
        high = max(r1 for _, _, r1 in tiles)
        span = LANES * (tiles[-1][0] + 1)
        mine, mine_w = coeffs[low:high, :], weighted[low:high, :]
        count = high - low
        over = (((1,), (1,)), ((), ()))
        at = 0
        for c0 in range(0, span, 256):
            c1 = min(c0 + 256, span)
            both = lax.dot_general(
                jnp.concatenate([mine, mine_w], axis=0), coeffs[c0:c1, :], over,
                preferred_element_type=F32,
            )
            other = lax.dot_general(mine, weighted[c0:c1, :], over, preferred_element_type=F32)
            gram, ham = both[:count], 0.5 * (both[count:] + other)
            for j, r0, r1 in tiles:
                if c0 <= LANES * j < c1:
                    cols = slice(LANES * j - c0, LANES * (j + 1) - c0)
                    part[at : at + r1 - r0, :] = gram[r0 - low : r1 - low, cols]
                    at += r1 - r0
                    part[at : at + r1 - r0, :] = ham[r0 - low : r1 - low, cols]
                    at += r1 - r0
        if at < part.shape[0]:
            part[at:, :] = jnp.zeros((part.shape[0] - at, LANES), F32)
        batches[i].begin()

    def collect(i):
        at = 0
        for j, r0, r1 in TILES[i]:
            cols = slice(LANES * j, LANES * (j + 1))
            s_full[r0:r1, cols] = batches[i].gath[at : at + r1 - r0, :]
            at += r1 - r0
            h_full[r0:r1, cols] = batches[i].gath[at : at + r1 - r0, :]
            at += r1 - r0

    def advance(*order):
        for i in order:
            batches[i].advance()
            if batches[i].stage == 4:
                collect(i)

    def place_columns():
        p = lax.broadcasted_iota(jnp.int32, (WIDE, 1), 0)
        k = p // deep
        dz = (k + 1) // 2 * (2 * lax.rem(k, 2) - 1)
        slot = lax.rem(my_z - dz + nz, nz) * deep + p - k * deep
        slot = jnp.where(p < SLOTS, slot, p)
        place[...] = (slot == lax.broadcasted_iota(jnp.int32, (WIDE, WIDE), 1)).astype(F32).astype(BF16)

    mu = mu_ref[0]
    down = lax.broadcasted_iota(jnp.int32, (LANES, LANES), 0)
    across = lax.broadcasted_iota(jnp.int32, (LANES, LANES), 1)

    def assemble(i):
        here = slice(LANES * i, LANES * (i + 1))
        for j in range(i + 1):
            there = slice(LANES * j, LANES * (j + 1))
            s_block, h_block = s_full[here, there], h_full[here, there]
            if i == j:
                s_block = jnp.where(down >= across, s_block, s_block.T)
                h_block = jnp.where(down >= across, h_block, h_block.T)
            l_block = -0.5 * (h_block - mu * s_block)
            if i == j:
                l_block = l_block + jnp.where(down == across, 0.5 * present[here, :], 0.0)
                s_full[here, there] = s_block
                h_full[here, there] = h_block
            else:
                s_full[there, here] = s_block.T
                h_full[there, here] = h_block.T
                l_block_t = l_block.T
                l_full[there, here] = l_block_t
                s_high[there, here], s_low[there, here] = split(s_block.T)
                l_high[there, here], l_low[there, here] = split(l_block_t)
            l_full[here, there] = l_block
            s_high[here, there], s_low[here, there] = split(s_block)
            l_high[here, there], l_low[here, there] = split(l_block)

    fill(1, 2)
    pl.semaphore_wait(barrier, n_fn - 1 + ny - 1 + NX - 1)
    every = range(CORES)
    z_start((1, 2), every)
    fill(3, 4)
    z_start((3, 4), every)
    fill(0)
    z_start((0,), every[1:])
    recv[me] = send[me]
    fill(*range(5, nz))
    coeffs[...] = jnp.zeros(coeffs.shape, BF16)
    weighted[...] = jnp.zeros(weighted.shape, BF16)
    place_columns()
    present[SLOTS:, :] = jnp.zeros((WIDE - SLOTS, LANES), F32)
    s_full[SLOTS:, :] = jnp.zeros((WIDE - SLOTS, WIDE), F32)
    h_full[SLOTS:, :] = jnp.zeros((WIDE - SLOTS, WIDE), F32)
    l_rows[...] = jnp.zeros(l_rows.shape, F32)
    half, other = every[:1], every[1:]
    z_left((1, 2), every)
    z_start((5, 6), half)
    z_left((3, 4), every)
    z_start((5, 6), other)
    unpack(0, 1, 2, 3, 4)
    share(0)
    z_left((5, 6), half)
    z_start((7, 8), half)
    z_left((5, 6), other)
    z_start((7, 8), other)
    unpack(5, 6)
    share(1)
    z_left((7, 8), half)
    z_start((9, 10), half)
    advance(0)
    z_left((7, 8), other)
    z_start((9, 10), other)
    unpack(7, 8)
    advance(1)
    share(2)
    advance(0)
    z_left((9, 10), half)
    z_start((11,), half)
    advance(1, 0)
    z_left((9, 10), other)
    z_start((11,), other)
    unpack(9, 10)
    share(3)
    advance(2, 1, 0, 2)
    unpack(11)
    share(4)
    advance(1, 3, 2, 4, 3, 4, 2, 3, 4, 3)
    for i in range(4):
        assemble(i)
    advance(4)
    assemble(4)

    count = packed.shape[1]
    room = l_rows.shape[1]
    for i in range(count):
        slot = blk * count + i
        chip = slot // deep
        dz = wrap(my_z - chip, nz)
        far = (dz + nz // 2 - 1) // nz
        k = (1 - far) * (2 * dz - (dz + nz - 1) // nz) + far * (2 * nz - 2 * dz)
        row = pl.ds(k * deep + slot - chip * deep, 1)
        l_rows[0, i : i + 1, :] = l_full[row, :]
        l_rows[1, i : i + 1, :] = s_full[row, :]
        l_rows[2, i : i + 1, :] = h_full[row, :]
    product = times(l_rows[0], s_high, s_low)
    square = times(product, l_high, l_low)
    cubed = times(times(square, s_high, s_low), l_high, l_low)

    result = jnp.concatenate([l_rows[1], l_rows[2], 3.0 * square - 2.0 * cubed], axis=0)
    high, rest = result.astype(BF16), result - result.astype(BF16).astype(F32)
    middle, low = split(rest)
    placed = jnp.dot(
        jnp.concatenate([high, middle, low], axis=0), place[...], preferred_element_type=F32
    )
    placed = placed[: 3 * room] + placed[3 * room : 6 * room] + placed[6 * room :]
    for i in range(3):
        packed[i] = placed[i * room : i * room + count, :SLOTS].reshape(count, 1, SLOTS)

    for k, dc in list(z_waiting):
        z_left((k,), (dc,))
    for batch in batches:
        batch.drain()


def hand_out(packed, *outs):
    for i, out in enumerate(outs):
        out[...] = packed[i]


def on_device(orbitals, potential, zone_of, chem_shift):
    n_fn = lax.axis_size("fn")
    n_blk = lax.axis_size("blk")
    ny = n_blk // NX
    cap = SLOTS // n_fn
    funcs, slab = orbitals.shape
    count = SLOTS // n_blk
    sizes = [
        -(-2 * sum(r1 - r0 for _, r0, r1 in tiles) // (n_blk * 8)) * 8 for tiles in TILES
    ]
    batch_scratch = []
    for size in sizes:
        batch_scratch += [
            pltpu.VMEM((n_blk * size, LANES), F32),
            pltpu.VMEM((n_blk * size, LANES), F32),
            pltpu.VMEM((max(1, NX - 1), ny * size, LANES), F32),
            pltpu.VMEM((ny - 1, size, LANES), F32),
        ] + [pltpu.SemaphoreType.DMA((2, max(1, n - 1))) for n in (NX, ny, ny, NX)]

    out = jax.ShapeDtypeStruct((count, 1, SLOTS), F32)
    vmem = pl.BlockSpec(memory_space=pltpu.VMEM)
    hbm = pl.BlockSpec(memory_space=pltpu.HBM)

    def body(*refs):
        kernel(n_fn, ny, sizes, *refs)

    packed = pl.pallas_call(
        body,
        out_shape=jax.ShapeDtypeStruct((3, count, 1, SLOTS), F32),
        in_specs=[hbm, hbm, hbm, pl.BlockSpec(memory_space=pltpu.SMEM)],
        out_specs=vmem,
        scratch_shapes=[
            pltpu.VMEM((1, funcs), jnp.int32),
            pltpu.VMEM((funcs, slab), BF16),
            pltpu.VMEM((1, slab), F32),
            pltpu.SemaphoreType.DMA((3,)),
            pltpu.VMEM((n_fn, cap, slab), BF16),
            pltpu.VMEM((n_fn, cap, slab), BF16),
            pltpu.VMEM((WIDE, slab), BF16),
            pltpu.VMEM((WIDE, slab), BF16),
            pltpu.VMEM((WIDE, LANES), F32),
            pltpu.VMEM((WIDE, WIDE), BF16),
            pltpu.VMEM((WIDE, WIDE), F32),
            pltpu.VMEM((WIDE, WIDE), F32),
            pltpu.VMEM((WIDE, WIDE), F32),
            pltpu.VMEM((WIDE, WIDE), BF16),
            pltpu.VMEM((WIDE, WIDE), BF16),
            pltpu.VMEM((WIDE, WIDE), BF16),
            pltpu.VMEM((WIDE, WIDE), BF16),
            pltpu.VMEM((3, -(-count // 16) * 16, WIDE), F32),
            pltpu.SemaphoreType.DMA((n_fn - 1,)),
            pltpu.SemaphoreType.DMA((n_fn - 1,)),
            *batch_scratch,
        ],
        compiler_params=pltpu.CompilerParams(
            collective_id=0, has_side_effects=True, vmem_limit_bytes=60 * 1024 * 1024
        ),
    )(zone_of.reshape(1, funcs), orbitals, potential, chem_shift)
    results = pl.pallas_call(
        hand_out,
        out_shape=(out, out, out),
        in_specs=[vmem],
        out_specs=(vmem, vmem, vmem),
    )(packed)
    return tuple(jnp.transpose(result, (1, 0, 2)) for result in results)


def solution(mesh):
    placed = (P("fn", "blk"), P("fn", "blk"), P("fn", None), P())
    return jax.shard_map(
        on_device,
        mesh=mesh,
        in_specs=placed,
        out_specs=(P("fn", "blk", None), P("fn", "blk", None), P("fn", "blk", None)),
        check_vma=False,
    )
```

```python
import jax
import jax.numpy as jnp
from jax import lax
from jax.experimental import pallas as pl
from jax.experimental.pallas import tpu as pltpu
from jax.sharding import PartitionSpec as P

SLOTS = 576
WIDE = 640
LANES = 128
NX = 4
CORES = 2
BIG = 2.0**100
BF16 = jnp.bfloat16
F32 = jnp.float32

TILES = [
    [(0, 0, 240), (1, 128, 240)],
    [(0, 240, 336), (1, 240, 336), (2, 272, 336)],
    [(0, 336, 432), (1, 336, 432), (2, 256, 272), (2, 336, 432), (3, 384, 432)],
    [(0, 432, 528), (1, 432, 528), (2, 432, 528), (3, 432, 528)],
    [(0, 528, 576), (1, 528, 576), (2, 528, 576), (3, 528, 576), (4, 512, 576)],
]


def wrap(value, n):
    return lax.rem(value + n, n)


def rows(start, count):
    return pl.ds(pl.multiple_of(start, 8), count)


def split(value):
    high = value.astype(BF16)
    return high, (value - high.astype(F32)).astype(BF16)


def times(left, right_high, right_low):
    high, low = split(left)
    count = left.shape[0]
    both = jnp.dot(
        jnp.concatenate([high, low], axis=0), right_high[...], preferred_element_type=F32
    )
    return both[:count] + both[count:] + jnp.dot(high, right_low[...], preferred_element_type=F32)


class Ring:
    def __init__(self, n, me, device, base, size):
        self.n, self.me, self.device, self.base, self.size = n, me, device, base, size

    def at(self, offset):
        return self.base + wrap(self.me + offset, self.n) * self.size


def far_first(n):
    return sorted(range(1, n), key=lambda k: -min(k, n - k))


def direct_sum(ring, data, total, landing, send_sem, recv_sem):
    copies = []

    def start():
        for k in far_first(ring.n):
            copies.append(
                pltpu.make_async_remote_copy(
                    src_ref=data.at[rows(ring.at(k), ring.size)],
                    dst_ref=landing.at[k - 1],
                    send_sem=send_sem.at[k - 1],
                    recv_sem=recv_sem.at[k - 1],
                    device_id=ring.device(wrap(ring.me + k, ring.n)),
                )
            )
            copies[-1].start()

    def finish():
        here = rows(ring.at(0), ring.size)
        value = data[here, :]
        for copy, k in zip(copies, far_first(ring.n)):
            copy.wait_recv()
            value = value + landing[k - 1]
        total[here, :] = value

    return start, finish, copies


def direct_gather(ring, data, send_sem, recv_sem):
    sent = []

    def copy(k, offset):
        here = data.at[rows(ring.at(offset), ring.size)]
        return pltpu.make_async_remote_copy(
            src_ref=here,
            dst_ref=here,
            send_sem=send_sem.at[k - 1],
            recv_sem=recv_sem.at[k - 1],
            device_id=ring.device(wrap(ring.me + k, ring.n)),
        )

    def start():
        for k in far_first(ring.n):
            sent.append(copy(k, 0))
            sent[-1].start()

    def finish():
        for k in far_first(ring.n):
            copy(k, -k).wait_recv()

    return start, finish, sent


class Batch:
    def __init__(self, n_x, n_y, x, y, along_x, along_y, size, refs):
        part, gath, land_x, land_y, sum_x, sum_y, get_y, get_x = refs
        self.part, self.gath = part, gath
        ring_x = Ring(n_x, x, along_x, 0, n_y * size)
        ring_y = Ring(n_y, y, along_y, x * (n_y * size), size)
        stages = [
            direct_sum(ring_x, part, part, land_x, sum_x.at[0], sum_x.at[1]),
            direct_sum(ring_y, part, gath, land_y, sum_y.at[0], sum_y.at[1]),
            direct_gather(ring_y, gath, get_y.at[0], get_y.at[1]),
            direct_gather(ring_x, gath, get_x.at[0], get_x.at[1]),
        ]
        self.starts = [s[0] for s in stages]
        self.finishes = [s[1] for s in stages]
        self.sent = [s[2] for s in stages]
        self.stage = 0

    def begin(self):
        self.starts[0]()

    def advance(self):
        self.finishes[self.stage]()
        self.stage += 1
        if self.stage < len(self.starts):
            self.starts[self.stage]()

    def drain(self, stages):
        for stage in stages:
            for copy in self.sent[stage]:
                copy.wait_send()


def kernel(
    n_fn, ny, sizes,
    zone_hbm, orb_hbm, pot_hbm, mu_ref, packed,
    zone_ref, orb_ref, pot_ref, in_sem, send, recv, coeffs, weighted, present, place,
    s_full, h_full, l_full, s_high, s_low, l_high, l_low, l_rows,
    z_send, z_recv, *batch_refs,
):
    cap = SLOTS // n_fn
    nz = n_fn // CORES
    deep = CORES * cap
    me = lax.axis_index("fn")
    blk = lax.axis_index("blk")
    my_z, core = me // CORES, lax.rem(me, CORES)
    y, x = blk // NX, lax.rem(blk, NX)

    def along_y(pos):
        return {"blk": pos * NX + x}

    def along_x(pos):
        return {"blk": y * NX + pos}

    def fn_index(dz, dc):
        return wrap(my_z + dz, nz) * CORES + lax.rem(core + dc, CORES)

    loads = [
        pltpu.make_async_copy(src, dst, in_sem.at[i])
        for i, (src, dst) in enumerate(
            ((zone_hbm, zone_ref), (orb_hbm, orb_ref), (pot_hbm, pot_ref))
        )
    ]
    for load in loads:
        load.start()

    barrier = pltpu.get_barrier_semaphore()

    @pl.loop(1, n_fn)
    def _(k):
        pl.semaphore_signal(barrier, inc=1, device_id={"fn": wrap(me + k - n_fn, n_fn)})

    for k in range(1, ny):
        pl.semaphore_signal(barrier, inc=1, device_id=along_y(wrap(y + k, ny)))
    for k in range(1, NX):
        pl.semaphore_signal(barrier, inc=1, device_id=along_x(wrap(x + k, NX)))

    loads[0].wait()
    funcs = orb_ref.shape[0]
    slab = orb_ref.shape[1]
    zones = zone_ref[...]
    onehot = (zones == lax.broadcasted_iota(jnp.int32, (n_fn, funcs), 0)).astype(F32)
    earlier = (
        lax.broadcasted_iota(jnp.int32, (funcs, funcs), 0)
        < lax.broadcasted_iota(jnp.int32, (funcs, funcs), 1)
    ).astype(F32)
    before = jnp.dot(onehot.astype(BF16), earlier.astype(BF16), preferred_element_type=F32)
    rank = jnp.sum(before * onehot, axis=0, keepdims=True).astype(jnp.int32)
    target = zones * cap + rank
    loads[1].wait()
    loads[2].wait()

    def near(k):
        return (k + 1) // 2 * (1 if k % 2 else -1)

    z_waiting = []

    def z_copy(k, dc, arriving):
        q = CORES * k + dc - 1
        to = fn_index(near(k), dc)
        return pltpu.make_async_remote_copy(
            src_ref=send.at[to],
            dst_ref=recv.at[fn_index(-near(k), dc) if arriving else me],
            send_sem=z_send.at[q],
            recv_sem=z_recv.at[q],
            device_id={"fn": to},
        )

    def z_start(chips, cores):
        for k in chips:
            for dc in cores:
                z_copy(k, dc, False).start()
                z_waiting.append((k, dc))

    def z_left(chips, cores):
        for k in chips:
            for dc in cores:
                z_copy(k, dc, False).wait_send()
                z_waiting.remove((k, dc))

    def fill(*chips):
        for k in chips:
            chip = wrap(my_z + near(k), nz)
            slot = lax.broadcasted_iota(jnp.int32, (deep, funcs), 0) + chip * deep
            selector = (target == slot).astype(F32)
            filled = jnp.sum(selector, axis=1, keepdims=True) > 0.5
            block = jnp.dot(selector.astype(BF16), orb_ref[...], preferred_element_type=F32)
            block = jnp.where(filled, block, BIG)
            for c in range(CORES):
                send[chip * CORES + c] = block[c * cap : (c + 1) * cap].astype(BF16)

    def unpack(*chips):
        for k in chips:
            for dc in range(0 if k else 1, CORES):
                z_copy(k, dc, True).wait_recv()
            chip = wrap(my_z - near(k), nz)
            value = jnp.concatenate(
                [recv[chip * CORES + c].astype(F32) for c in range(CORES)], axis=0
            )
            marks = value[:, :1] < 0.5 * BIG
            value = jnp.where(marks, value, 0.0)
            here = slice(k * deep, (k + 1) * deep)
            coeffs[here, :] = value.astype(BF16)
            weighted[here, :] = (pot_ref[...] * value).astype(BF16)
            present[here, :] = jnp.broadcast_to(marks.astype(F32), (deep, LANES))

    batches = [
        Batch(NX, ny, x, y, along_x, along_y, size, batch_refs[8 * i : 8 * i + 8])
        for i, size in enumerate(sizes)
    ]

    def share(i):
        part = batches[i].part
        tiles = TILES[i]
        low = min(r0 for _, r0, _ in tiles)
        high = max(r1 for _, _, r1 in tiles)
        span = LANES * (tiles[-1][0] + 1)
        mine, mine_w = coeffs[low:high, :], weighted[low:high, :]
        count = high - low
        over = (((1,), (1,)), ((), ()))
        at = 0
        for c0 in range(0, span, 256):
            c1 = min(c0 + 256, span)
            both = lax.dot_general(
                jnp.concatenate([mine, mine_w], axis=0), coeffs[c0:c1, :], over,
                preferred_element_type=F32,
            )
            other = lax.dot_general(mine, weighted[c0:c1, :], over, preferred_element_type=F32)
            gram, ham = both[:count], 0.5 * (both[count:] + other)
            for j, r0, r1 in tiles:
                if c0 <= LANES * j < c1:
                    cols = slice(LANES * j - c0, LANES * (j + 1) - c0)
                    part[at : at + r1 - r0, :] = gram[r0 - low : r1 - low, cols]
                    at += r1 - r0
                    part[at : at + r1 - r0, :] = ham[r0 - low : r1 - low, cols]
                    at += r1 - r0
        if at < part.shape[0]:
            part[at:, :] = jnp.zeros((part.shape[0] - at, LANES), F32)
        batches[i].begin()

    def collect(i):
        at = 0
        for j, r0, r1 in TILES[i]:
            cols = slice(LANES * j, LANES * (j + 1))
            s_full[r0:r1, cols] = batches[i].gath[at : at + r1 - r0, :]
            at += r1 - r0
            h_full[r0:r1, cols] = batches[i].gath[at : at + r1 - r0, :]
            at += r1 - r0

    def advance(*order):
        for i in order:
            batches[i].advance()
            if batches[i].stage == 4:
                collect(i)

    def place_columns():
        p = lax.broadcasted_iota(jnp.int32, (WIDE, 1), 0)
        k = p // deep
        dz = (k + 1) // 2 * (2 * lax.rem(k, 2) - 1)
        slot = lax.rem(my_z - dz + nz, nz) * deep + p - k * deep
        slot = jnp.where(p < SLOTS, slot, p)
        place[...] = (slot == lax.broadcasted_iota(jnp.int32, (WIDE, WIDE), 1)).astype(F32).astype(BF16)

    mu = mu_ref[0]
    down = lax.broadcasted_iota(jnp.int32, (LANES, LANES), 0)
    across = lax.broadcasted_iota(jnp.int32, (LANES, LANES), 1)

    def assemble(i):
        here = slice(LANES * i, LANES * (i + 1))
        for j in range(i + 1):
            there = slice(LANES * j, LANES * (j + 1))
            s_block, h_block = s_full[here, there], h_full[here, there]
            if i == j:
                s_block = jnp.where(down >= across, s_block, s_block.T)
                h_block = jnp.where(down >= across, h_block, h_block.T)
            l_block = -0.5 * (h_block - mu * s_block)
            if i == j:
                l_block = l_block + jnp.where(down == across, 0.5 * present[here, :], 0.0)
                s_full[here, there] = s_block
                h_full[here, there] = h_block
            else:
                s_full[there, here] = s_block.T
                h_full[there, here] = h_block.T
                l_block_t = l_block.T
                l_full[there, here] = l_block_t
                s_high[there, here], s_low[there, here] = split(s_block.T)
                l_high[there, here], l_low[there, here] = split(l_block_t)
            l_full[here, there] = l_block
            s_high[here, there], s_low[here, there] = split(s_block)
            l_high[here, there], l_low[here, there] = split(l_block)

    fill(1, 2)
    pl.semaphore_wait(barrier, n_fn - 1 + ny - 1 + NX - 1)
    every = range(CORES)
    z_start((1, 2), every)
    fill(3, 4)
    z_start((3, 4), every)
    fill(0)
    z_start((0,), every[1:])
    recv[me] = send[me]
    fill(*range(5, nz))
    coeffs[...] = jnp.zeros(coeffs.shape, BF16)
    weighted[...] = jnp.zeros(weighted.shape, BF16)
    place_columns()
    present[SLOTS:, :] = jnp.zeros((WIDE - SLOTS, LANES), F32)
    s_full[SLOTS:, :] = jnp.zeros((WIDE - SLOTS, WIDE), F32)
    h_full[SLOTS:, :] = jnp.zeros((WIDE - SLOTS, WIDE), F32)
    l_rows[...] = jnp.zeros(l_rows.shape, F32)
    half, other = every[:1], every[1:]
    z_left((1, 2), every)
    z_start((5, 6), half)
    z_left((3, 4), every)
    z_start((5, 6), other)
    unpack(0, 1, 2, 3, 4)
    share(0)
    z_left((5, 6), half)
    z_start((7, 8), half)
    z_left((5, 6), other)
    z_start((7, 8), other)
    unpack(5, 6)
    share(1)
    z_left((7, 8), half)
    z_start((9, 10), half)
    advance(0)
    z_left((7, 8), other)
    z_start((9, 10), other)
    unpack(7, 8)
    advance(1)
    share(2)
    advance(0)
    z_left((9, 10), half)
    z_start((11,), half)
    advance(1, 0)
    z_left((9, 10), other)
    z_start((11,), other)
    unpack(9, 10)
    share(3)
    advance(2, 0)
    unpack(11)
    share(4)
    advance(1, 2, 3, 4, 1, 2, 3, 4, 3, 2, 4, 3)
    for i in range(4):
        assemble(i)
    for k, dc in list(z_waiting):
        z_left((k,), (dc,))
    for batch in batches[:4]:
        batch.drain(range(4))
    batches[4].drain(range(3))
    advance(4)
    assemble(4)

    count = packed.shape[1]
    room = l_rows.shape[1]
    for i in range(count):
        slot = blk * count + i
        chip = slot // deep
        dz = wrap(my_z - chip, nz)
        far = (dz + nz // 2 - 1) // nz
        k = (1 - far) * (2 * dz - (dz + nz - 1) // nz) + far * (2 * nz - 2 * dz)
        row = pl.ds(k * deep + slot - chip * deep, 1)
        l_rows[0, i : i + 1, :] = l_full[row, :]
        l_rows[1, i : i + 1, :] = s_full[row, :]
        l_rows[2, i : i + 1, :] = h_full[row, :]
    product = times(l_rows[0], s_high, s_low)
    square = times(product, l_high, l_low)
    cubed = times(times(square, s_high, s_low), l_high, l_low)

    result = jnp.concatenate([l_rows[1], l_rows[2], 3.0 * square - 2.0 * cubed], axis=0)
    high, rest = result.astype(BF16), result - result.astype(BF16).astype(F32)
    middle, low = split(rest)
    placed = jnp.dot(
        jnp.concatenate([high, middle, low], axis=0), place[...], preferred_element_type=F32
    )
    placed = placed[: 3 * room] + placed[3 * room : 6 * room] + placed[6 * room :]
    for i in range(3):
        packed[i] = placed[i * room : i * room + count, :SLOTS].reshape(count, 1, SLOTS)

    batches[4].drain((3,))


def hand_out(packed, *outs):
    for i, out in enumerate(outs):
        out[...] = packed[i]


def on_device(orbitals, potential, zone_of, chem_shift):
    n_fn = lax.axis_size("fn")
    n_blk = lax.axis_size("blk")
    ny = n_blk // NX
    cap = SLOTS // n_fn
    funcs, slab = orbitals.shape
    count = SLOTS // n_blk
    sizes = [
        -(-2 * sum(r1 - r0 for _, r0, r1 in tiles) // (n_blk * 8)) * 8 for tiles in TILES
    ]
    batch_scratch = []
    for size in sizes:
        batch_scratch += [
            pltpu.VMEM((n_blk * size, LANES), F32),
            pltpu.VMEM((n_blk * size, LANES), F32),
            pltpu.VMEM((max(1, NX - 1), ny * size, LANES), F32),
            pltpu.VMEM((ny - 1, size, LANES), F32),
        ] + [pltpu.SemaphoreType.DMA((2, max(1, n - 1))) for n in (NX, ny, ny, NX)]

    out = jax.ShapeDtypeStruct((count, 1, SLOTS), F32)
    vmem = pl.BlockSpec(memory_space=pltpu.VMEM)
    hbm = pl.BlockSpec(memory_space=pltpu.HBM)

    def body(*refs):
        kernel(n_fn, ny, sizes, *refs)

    packed = pl.pallas_call(
        body,
        out_shape=jax.ShapeDtypeStruct((3, count, 1, SLOTS), F32),
        in_specs=[hbm, hbm, hbm, pl.BlockSpec(memory_space=pltpu.SMEM)],
        out_specs=vmem,
        scratch_shapes=[
            pltpu.VMEM((1, funcs), jnp.int32),
            pltpu.VMEM((funcs, slab), BF16),
            pltpu.VMEM((1, slab), F32),
            pltpu.SemaphoreType.DMA((3,)),
            pltpu.VMEM((n_fn, cap, slab), BF16),
            pltpu.VMEM((n_fn, cap, slab), BF16),
            pltpu.VMEM((WIDE, slab), BF16),
            pltpu.VMEM((WIDE, slab), BF16),
            pltpu.VMEM((WIDE, LANES), F32),
            pltpu.VMEM((WIDE, WIDE), BF16),
            pltpu.VMEM((WIDE, WIDE), F32),
            pltpu.VMEM((WIDE, WIDE), F32),
            pltpu.VMEM((WIDE, WIDE), F32),
            pltpu.VMEM((WIDE, WIDE), BF16),
            pltpu.VMEM((WIDE, WIDE), BF16),
            pltpu.VMEM((WIDE, WIDE), BF16),
            pltpu.VMEM((WIDE, WIDE), BF16),
            pltpu.VMEM((3, -(-count // 16) * 16, WIDE), F32),
            pltpu.SemaphoreType.DMA((n_fn - 1,)),
            pltpu.SemaphoreType.DMA((n_fn - 1,)),
            *batch_scratch,
        ],
        compiler_params=pltpu.CompilerParams(
            collective_id=0, has_side_effects=True, vmem_limit_bytes=60 * 1024 * 1024
        ),
    )(zone_of.reshape(1, funcs), orbitals, potential, chem_shift)
    results = pl.pallas_call(
        hand_out,
        out_shape=(out, out, out),
        in_specs=[vmem],
        out_specs=(vmem, vmem, vmem),
    )(packed)
    return tuple(jnp.transpose(result, (1, 0, 2)) for result in results)


def solution(mesh):
    placed = (P("fn", "blk"), P("fn", "blk"), P("fn", None), P())
    return jax.shard_map(
        on_device,
        mesh=mesh,
        in_specs=placed,
        out_specs=(P("fn", "blk", None), P("fn", "blk", None), P("fn", "blk", None)),
        check_vma=False,
    )
```

```python
import jax
import jax.numpy as jnp
from jax import lax
from jax.experimental import pallas as pl
from jax.experimental.pallas import tpu as pltpu
from jax.sharding import PartitionSpec as P

SLOTS = 576
WIDE = 640
LANES = 128
NX = 4
CORES = 2
BIG = 2.0**100
BF16 = jnp.bfloat16
F32 = jnp.float32

TILES = [
    [(0, 0, 240), (1, 128, 240)],
    [(0, 240, 336), (1, 240, 336), (2, 272, 336)],
    [(0, 336, 432), (1, 336, 432), (2, 256, 272), (2, 336, 432), (3, 384, 432)],
    [(0, 432, 528), (1, 432, 528), (2, 432, 528), (3, 432, 528)],
    [(0, 528, 576), (1, 528, 576), (2, 528, 576), (3, 528, 576), (4, 512, 576)],
]


def wrap(value, n):
    return lax.rem(value + n, n)


def rows(start, count):
    return pl.ds(pl.multiple_of(start, 8), count)


def split(value):
    high = value.astype(BF16)
    return high, (value - high.astype(F32)).astype(BF16)


def times(left, right_high, right_low):
    high, low = split(left)
    count = left.shape[0]
    both = jnp.dot(
        jnp.concatenate([high, low], axis=0), right_high[...], preferred_element_type=F32
    )
    return both[:count] + both[count:] + jnp.dot(high, right_low[...], preferred_element_type=F32)


class Ring:
    def __init__(self, n, me, device, base, size):
        self.n, self.me, self.device, self.base, self.size = n, me, device, base, size

    def at(self, offset):
        return self.base + wrap(self.me + offset, self.n) * self.size


def far_first(n):
    return sorted(range(1, n), key=lambda k: -min(k, n - k))


def direct_sum(ring, data, total, landing, send_sem, recv_sem):
    copies = []

    def start():
        for k in far_first(ring.n):
            copies.append(
                pltpu.make_async_remote_copy(
                    src_ref=data.at[rows(ring.at(k), ring.size)],
                    dst_ref=landing.at[k - 1],
                    send_sem=send_sem.at[k - 1],
                    recv_sem=recv_sem.at[k - 1],
                    device_id=ring.device(wrap(ring.me + k, ring.n)),
                )
            )
            copies[-1].start()

    def finish():
        here = rows(ring.at(0), ring.size)
        value = data[here, :]
        for copy, k in zip(copies, far_first(ring.n)):
            copy.wait_recv()
            value = value + landing[k - 1]
        total[here, :] = value

    return start, finish, copies


def direct_gather(ring, data, send_sem, recv_sem):
    sent = []

    def copy(k, offset):
        here = data.at[rows(ring.at(offset), ring.size)]
        return pltpu.make_async_remote_copy(
            src_ref=here,
            dst_ref=here,
            send_sem=send_sem.at[k - 1],
            recv_sem=recv_sem.at[k - 1],
            device_id=ring.device(wrap(ring.me + k, ring.n)),
        )

    def start():
        for k in far_first(ring.n):
            sent.append(copy(k, 0))
            sent[-1].start()

    def finish():
        for k in far_first(ring.n):
            copy(k, -k).wait_recv()

    return start, finish, sent


class Batch:
    def __init__(self, n_x, n_y, x, y, along_x, along_y, size, refs):
        part, gath, land_x, land_y, sum_x, sum_y, get_y, get_x = refs
        self.part, self.gath = part, gath
        ring_x = Ring(n_x, x, along_x, 0, n_y * size)
        ring_y = Ring(n_y, y, along_y, x * (n_y * size), size)
        stages = [
            direct_sum(ring_x, part, part, land_x, sum_x.at[0], sum_x.at[1]),
            direct_sum(ring_y, part, gath, land_y, sum_y.at[0], sum_y.at[1]),
            direct_gather(ring_y, gath, get_y.at[0], get_y.at[1]),
            direct_gather(ring_x, gath, get_x.at[0], get_x.at[1]),
        ]
        self.starts = [s[0] for s in stages]
        self.finishes = [s[1] for s in stages]
        self.sent = [s[2] for s in stages]
        self.stage = 0

    def begin(self):
        self.starts[0]()

    def advance(self):
        self.finishes[self.stage]()
        self.stage += 1
        if self.stage < len(self.starts):
            self.starts[self.stage]()

    def drain(self, stages):
        for stage in stages:
            for copy in self.sent[stage]:
                copy.wait_send()


def kernel(
    n_fn, ny, sizes,
    zone_hbm, orb_hbm, pot_hbm, mu_ref, packed,
    zone_ref, orb_ref, pot_ref, in_sem, send, recv, coeffs, weighted, present, place,
    s_full, h_full, l_full, s_high, s_low, l_high, l_low, l_rows,
    z_send, z_recv, *batch_refs,
):
    cap = SLOTS // n_fn
    nz = n_fn // CORES
    deep = CORES * cap
    me = lax.axis_index("fn")
    blk = lax.axis_index("blk")
    my_z, core = me // CORES, lax.rem(me, CORES)
    y, x = blk // NX, lax.rem(blk, NX)

    def along_y(pos):
        return {"blk": pos * NX + x}

    def along_x(pos):
        return {"blk": y * NX + pos}

    def fn_index(dz, dc):
        return wrap(my_z + dz, nz) * CORES + lax.rem(core + dc, CORES)

    loads = [
        pltpu.make_async_copy(src, dst, in_sem.at[i])
        for i, (src, dst) in enumerate(
            ((zone_hbm, zone_ref), (orb_hbm, orb_ref), (pot_hbm, pot_ref))
        )
    ]
    for load in loads:
        load.start()

    barrier = pltpu.get_barrier_semaphore()

    @pl.loop(1, n_fn)
    def _(k):
        pl.semaphore_signal(barrier, inc=1, device_id={"fn": wrap(me + k - n_fn, n_fn)})

    for k in range(1, ny):
        pl.semaphore_signal(barrier, inc=1, device_id=along_y(wrap(y + k, ny)))
    for k in range(1, NX):
        pl.semaphore_signal(barrier, inc=1, device_id=along_x(wrap(x + k, NX)))

    loads[0].wait()
    funcs = orb_ref.shape[0]
    slab = orb_ref.shape[1]
    zones = zone_ref[...]
    onehot = (zones == lax.broadcasted_iota(jnp.int32, (n_fn, funcs), 0)).astype(F32)
    earlier = (
        lax.broadcasted_iota(jnp.int32, (funcs, funcs), 0)
        < lax.broadcasted_iota(jnp.int32, (funcs, funcs), 1)
    ).astype(F32)
    before = jnp.dot(onehot.astype(BF16), earlier.astype(BF16), preferred_element_type=F32)
    rank = jnp.sum(before * onehot, axis=0, keepdims=True).astype(jnp.int32)
    target = zones * cap + rank
    loads[1].wait()
    loads[2].wait()

    def near(k):
        return (k + 1) // 2 * (1 if k % 2 else -1)

    z_waiting = []

    def z_copy(k, dc, arriving):
        q = CORES * k + dc - 1
        to = fn_index(near(k), dc)
        return pltpu.make_async_remote_copy(
            src_ref=send.at[to],
            dst_ref=recv.at[fn_index(-near(k), dc) if arriving else me],
            send_sem=z_send.at[q],
            recv_sem=z_recv.at[q],
            device_id={"fn": to},
        )

    def z_start(chips, cores):
        for k in chips:
            for dc in cores:
                z_copy(k, dc, False).start()
                z_waiting.append((k, dc))

    def z_left(chips, cores):
        for k in chips:
            for dc in cores:
                z_copy(k, dc, False).wait_send()
                z_waiting.remove((k, dc))

    def fill(*chips):
        for k in chips:
            chip = wrap(my_z + near(k), nz)
            slot = lax.broadcasted_iota(jnp.int32, (deep, funcs), 0) + chip * deep
            selector = (target == slot).astype(F32)
            filled = jnp.sum(selector, axis=1, keepdims=True) > 0.5
            block = jnp.dot(selector.astype(BF16), orb_ref[...], preferred_element_type=F32)
            block = jnp.where(filled, block, BIG)
            for c in range(CORES):
                send[chip * CORES + c] = block[c * cap : (c + 1) * cap].astype(BF16)

    def unpack(*chips):
        for k in chips:
            for dc in range(0 if k else 1, CORES):
                z_copy(k, dc, True).wait_recv()
            chip = wrap(my_z - near(k), nz)
            value = jnp.concatenate(
                [recv[chip * CORES + c].astype(F32) for c in range(CORES)], axis=0
            )
            marks = value[:, :1] < 0.5 * BIG
            value = jnp.where(marks, value, 0.0)
            here = slice(k * deep, (k + 1) * deep)
            coeffs[here, :] = value.astype(BF16)
            weighted[here, :] = (pot_ref[...] * value).astype(BF16)
            present[here, :] = jnp.broadcast_to(marks.astype(F32), (deep, LANES))

    batches = [
        Batch(NX, ny, x, y, along_x, along_y, size, batch_refs[8 * i : 8 * i + 8])
        for i, size in enumerate(sizes)
    ]

    def share(i):
        part = batches[i].part
        tiles = TILES[i]
        low = min(r0 for _, r0, _ in tiles)
        high = max(r1 for _, _, r1 in tiles)
        span = LANES * (tiles[-1][0] + 1)
        mine, mine_w = coeffs[low:high, :], weighted[low:high, :]
        count = high - low
        over = (((1,), (1,)), ((), ()))
        at = 0
        for c0 in range(0, span, 256):
            c1 = min(c0 + 256, span)
            both = lax.dot_general(
                jnp.concatenate([mine, mine_w], axis=0), coeffs[c0:c1, :], over,
                preferred_element_type=F32,
            )
            other = lax.dot_general(mine, weighted[c0:c1, :], over, preferred_element_type=F32)
            gram, ham = both[:count], 0.5 * (both[count:] + other)
            for j, r0, r1 in tiles:
                if c0 <= LANES * j < c1:
                    cols = slice(LANES * j - c0, LANES * (j + 1) - c0)
                    part[at : at + r1 - r0, :] = gram[r0 - low : r1 - low, cols]
                    at += r1 - r0
                    part[at : at + r1 - r0, :] = ham[r0 - low : r1 - low, cols]
                    at += r1 - r0
        if at < part.shape[0]:
            part[at:, :] = jnp.zeros((part.shape[0] - at, LANES), F32)
        batches[i].begin()

    def collect(i):
        at = 0
        for j, r0, r1 in TILES[i]:
            cols = slice(LANES * j, LANES * (j + 1))
            s_full[r0:r1, cols] = batches[i].gath[at : at + r1 - r0, :]
            at += r1 - r0
            h_full[r0:r1, cols] = batches[i].gath[at : at + r1 - r0, :]
            at += r1 - r0

    def advance(*order):
        for i in order:
            batches[i].advance()
            if batches[i].stage == 4:
                collect(i)

    def place_columns():
        p = lax.broadcasted_iota(jnp.int32, (WIDE, 1), 0)
        k = p // deep
        dz = (k + 1) // 2 * (2 * lax.rem(k, 2) - 1)
        slot = lax.rem(my_z - dz + nz, nz) * deep + p - k * deep
        slot = jnp.where(p < SLOTS, slot, p)
        place[...] = (slot == lax.broadcasted_iota(jnp.int32, (WIDE, WIDE), 1)).astype(F32).astype(BF16)

    mu = mu_ref[0]
    down = lax.broadcasted_iota(jnp.int32, (LANES, LANES), 0)
    across = lax.broadcasted_iota(jnp.int32, (LANES, LANES), 1)

    def assemble(i):
        here = slice(LANES * i, LANES * (i + 1))
        for j in range(i + 1):
            there = slice(LANES * j, LANES * (j + 1))
            s_block, h_block = s_full[here, there], h_full[here, there]
            if i == j:
                s_block = jnp.where(down >= across, s_block, s_block.T)
                h_block = jnp.where(down >= across, h_block, h_block.T)
            l_block = -0.5 * (h_block - mu * s_block)
            if i == j:
                l_block = l_block + jnp.where(down == across, 0.5 * present[here, :], 0.0)
                s_full[here, there] = s_block
                h_full[here, there] = h_block
            else:
                s_full[there, here] = s_block.T
                h_full[there, here] = h_block.T
                l_block_t = l_block.T
                l_full[there, here] = l_block_t
                s_high[there, here], s_low[there, here] = split(s_block.T)
                l_high[there, here], l_low[there, here] = split(l_block_t)
            l_full[here, there] = l_block
            s_high[here, there], s_low[here, there] = split(s_block)
            l_high[here, there], l_low[here, there] = split(l_block)

    fill(1, 2)
    pl.semaphore_wait(barrier, n_fn - 1 + ny - 1 + NX - 1)
    every = range(CORES)
    z_start((1, 2), every)
    fill(3, 4)
    z_start((3, 4), every)
    fill(0)
    z_start((0,), every[1:])
    recv[me] = send[me]
    half, other = every[:1], every[1:]
    fill(5, 6)
    z_left((1, 2), every)
    z_start((5, 6), half)
    fill(*range(7, nz))
    z_left((3, 4), every)
    z_start((5, 6), other)
    coeffs[...] = jnp.zeros(coeffs.shape, BF16)
    weighted[...] = jnp.zeros(weighted.shape, BF16)
    place_columns()
    present[SLOTS:, :] = jnp.zeros((WIDE - SLOTS, LANES), F32)
    s_full[SLOTS:, :] = jnp.zeros((WIDE - SLOTS, WIDE), F32)
    h_full[SLOTS:, :] = jnp.zeros((WIDE - SLOTS, WIDE), F32)
    l_rows[...] = jnp.zeros(l_rows.shape, F32)
    unpack(0, 1, 2, 3, 4)
    share(0)
    z_left((5, 6), half)
    z_start((7, 8), half)
    z_left((5, 6), other)
    z_start((7, 8), other)
    unpack(5, 6)
    share(1)
    z_left((7, 8), half)
    z_start((9, 10), half)
    advance(0)
    z_left((7, 8), other)
    z_start((9, 10), other)
    unpack(7, 8)
    advance(1)
    share(2)
    advance(0)
    z_left((9, 10), half)
    z_start((11,), half)
    advance(1, 0)
    z_left((9, 10), other)
    z_start((11,), other)
    unpack(9, 10)
    share(3)
    advance(2, 0)
    unpack(11)
    share(4)
    advance(1, 2, 3, 4, 1, 2, 3, 4, 3, 2, 4, 3)
    for i in range(4):
        assemble(i)
    for k, dc in list(z_waiting):
        z_left((k,), (dc,))
    for batch in batches[:4]:
        batch.drain(range(4))
    batches[4].drain(range(3))
    advance(4)
    assemble(4)

    count = packed.shape[1]
    room = l_rows.shape[1]
    for i in range(count):
        slot = blk * count + i
        chip = slot // deep
        dz = wrap(my_z - chip, nz)
        far = (dz + nz // 2 - 1) // nz
        k = (1 - far) * (2 * dz - (dz + nz - 1) // nz) + far * (2 * nz - 2 * dz)
        row = pl.ds(k * deep + slot - chip * deep, 1)
        l_rows[0, i : i + 1, :] = l_full[row, :]
        l_rows[1, i : i + 1, :] = s_full[row, :]
        l_rows[2, i : i + 1, :] = h_full[row, :]
    product = times(l_rows[0], s_high, s_low)
    square = times(product, l_high, l_low)
    cubed = times(times(square, s_high, s_low), l_high, l_low)

    result = jnp.concatenate([l_rows[1], l_rows[2], 3.0 * square - 2.0 * cubed], axis=0)
    high, rest = result.astype(BF16), result - result.astype(BF16).astype(F32)
    middle, low = split(rest)
    placed = jnp.dot(
        jnp.concatenate([high, middle, low], axis=0), place[...], preferred_element_type=F32
    )
    placed = placed[: 3 * room] + placed[3 * room : 6 * room] + placed[6 * room :]
    for i in range(3):
        packed[i] = placed[i * room : i * room + count, :SLOTS].reshape(count, 1, SLOTS)

    batches[4].drain((3,))


def hand_out(packed, *outs):
    for i, out in enumerate(outs):
        out[...] = packed[i]


def on_device(orbitals, potential, zone_of, chem_shift):
    n_fn = lax.axis_size("fn")
    n_blk = lax.axis_size("blk")
    ny = n_blk // NX
    cap = SLOTS // n_fn
    funcs, slab = orbitals.shape
    count = SLOTS // n_blk
    sizes = [
        -(-2 * sum(r1 - r0 for _, r0, r1 in tiles) // (n_blk * 8)) * 8 for tiles in TILES
    ]
    batch_scratch = []
    for size in sizes:
        batch_scratch += [
            pltpu.VMEM((n_blk * size, LANES), F32),
            pltpu.VMEM((n_blk * size, LANES), F32),
            pltpu.VMEM((max(1, NX - 1), ny * size, LANES), F32),
            pltpu.VMEM((ny - 1, size, LANES), F32),
        ] + [pltpu.SemaphoreType.DMA((2, max(1, n - 1))) for n in (NX, ny, ny, NX)]

    out = jax.ShapeDtypeStruct((count, 1, SLOTS), F32)
    vmem = pl.BlockSpec(memory_space=pltpu.VMEM)
    hbm = pl.BlockSpec(memory_space=pltpu.HBM)

    def body(*refs):
        kernel(n_fn, ny, sizes, *refs)

    packed = pl.pallas_call(
        body,
        out_shape=jax.ShapeDtypeStruct((3, count, 1, SLOTS), F32),
        in_specs=[hbm, hbm, hbm, pl.BlockSpec(memory_space=pltpu.SMEM)],
        out_specs=vmem,
        scratch_shapes=[
            pltpu.VMEM((1, funcs), jnp.int32),
            pltpu.VMEM((funcs, slab), BF16),
            pltpu.VMEM((1, slab), F32),
            pltpu.SemaphoreType.DMA((3,)),
            pltpu.VMEM((n_fn, cap, slab), BF16),
            pltpu.VMEM((n_fn, cap, slab), BF16),
            pltpu.VMEM((WIDE, slab), BF16),
            pltpu.VMEM((WIDE, slab), BF16),
            pltpu.VMEM((WIDE, LANES), F32),
            pltpu.VMEM((WIDE, WIDE), BF16),
            pltpu.VMEM((WIDE, WIDE), F32),
            pltpu.VMEM((WIDE, WIDE), F32),
            pltpu.VMEM((WIDE, WIDE), F32),
            pltpu.VMEM((WIDE, WIDE), BF16),
            pltpu.VMEM((WIDE, WIDE), BF16),
            pltpu.VMEM((WIDE, WIDE), BF16),
            pltpu.VMEM((WIDE, WIDE), BF16),
            pltpu.VMEM((3, -(-count // 16) * 16, WIDE), F32),
            pltpu.SemaphoreType.DMA((n_fn - 1,)),
            pltpu.SemaphoreType.DMA((n_fn - 1,)),
            *batch_scratch,
        ],
        compiler_params=pltpu.CompilerParams(
            collective_id=0, has_side_effects=True, vmem_limit_bytes=60 * 1024 * 1024
        ),
    )(zone_of.reshape(1, funcs), orbitals, potential, chem_shift)
    results = pl.pallas_call(
        hand_out,
        out_shape=(out, out, out),
        in_specs=[vmem],
        out_specs=(vmem, vmem, vmem),
    )(packed)
    return tuple(jnp.transpose(result, (1, 0, 2)) for result in results)


def solution(mesh):
    placed = (P("fn", "blk"), P("fn", "blk"), P("fn", None), P())
    return jax.shard_map(
        on_device,
        mesh=mesh,
        in_specs=placed,
        out_specs=(P("fn", "blk", None), P("fn", "blk", None), P("fn", "blk", None)),
        check_vma=False,
    )
```
